32 devices in a mesh: groups: 2 (over x), wide: 8 (over z, y), tp: 2 (over core).
Axes of the slice: x: 2, y: 2, z: 4, core: 2. Of those that a mesh axis runs over, the one named last changes fastest.
Arguments:
- normed_layer_input: bfloat16 [512, 8192], P(('groups', 'wide')), parts along dimension 0, may hold values from -6 to 6
- plain_query_rows: bfloat16 [512, 8192], P(('groups', 'wide'), 'tp'), parts along dimension 0, may hold values from -10 to 10
- plain_key_rows: bfloat16 [512, 1024], P(('groups', 'wide'), 'tp'), parts along dimension 0, may hold values from -6 to 6
- plain_value_rows: bfloat16 [512, 1024], P(('groups', 'wide'), 'tp'), parts along dimension 0, may hold values from -6 to 6
- cached_key_rows: bfloat16 [512, 8, 96, 128], P(('groups', 'wide'), 'tp'), parts along dimension 0, may hold values from -61 to 61
- cached_value_rows: bfloat16 [512, 8, 96, 128], P(('groups', 'wide'), 'tp'), parts along dimension 0, may hold values from -6 to 6
- live_cache_length: int32 [512], P(('groups', 'wide')), parts along dimension 0, may hold values from 2 to 96, as said below
- tenant: int32 [512], P('groups'), parts along dimension 0, may hold values from 0 to 7, as said below
- slot_of_adapter: int32 [16], P('groups'), parts along dimension 0, may hold values from 0 to 7, as said below
- stacked_down_weight: bfloat16 [8, 192, 8192], P('wide'), may hold values from -0.0625 to 0.0625
- query_up_weight: bfloat16 [8, 64, 8192], P('wide', None, 'tp'), may hold values from -0.75 to 0.75
- key_value_up_weight: bfloat16 [8, 2, 64, 1024], P('wide', None, None, 'tp'), may hold values from -0.75 to 0.75
- output_down_weight: bfloat16 [8, 64, 8192], P('wide', None, 'tp'), may hold values from -0.375 to 0.375
- output_up_weight: bfloat16 [8, 64, 8192], P('wide', None, 'tp'), may hold values from -0.75 to 0.75
Outputs:
- context: bfloat16 [512, 8192], P(('groups', 'wide'), 'tp'), parts along dimension 0
- adapter_output_term: bfloat16 [512, 8192], P(('groups', 'wide'), 'tp'), parts along dimension 0
The draws below stay inside these ranges and needn't reach their ends.
There are 2 independent parts, one for each index of `groups`. The reference program is written for one: setup_inputs(seed, part) draws one part's arguments, and reference() takes and returns one part's arrays. A program takes and returns all parts, laid end to end along the dimension named above; an argument that names none is the same for every part. Nothing has to cross between parts.
Inputs may be any that keep to these rules, and one draw needn't show every extreme that they name: `tenant`: within each aligned block of 32 rows (the rows of one device along wide) no adapter is used by more than 8 rows, and one adapter is used by exactly 8 rows of every block. `slot_of_adapter`: A permutation; the slot of index s lies on the device of index s along wide. `live_cache_length`: every aligned block of 32 rows has a row with 96.
All inputs are finite; a program needn't handle non-finite values.
Results may differ from the reference program's by a relative error of at most 0.0095.
Values may be sent and summed in bfloat16 or wider, within the bound.
No kernel may reach another device: no remote copies, remote signals or barrier semaphores. Data moves between devices by JAX's collectives and lax.ppermute only.
A program may use at most 64 MiB of HBM per device.

```python
import jax
import jax.numpy as jnp
from jax import lax

MODEL_WIDTH = 8192
HEADS = 64
KV_HEADS = 8
HEAD_DIM = 128
ADAPTER_RANK = 64
ROW_DEV = 32
CACHE = 96
KEY_FEATURES = 1024
ROWS = 256
ADAPTER_SLOTS = 8
CAP = 8
N_WIDE = 8


def query_noise(key):
    return jax.random.truncated_normal(key, -4.0, 4.0, (ROWS, MODEL_WIDTH), jnp.float32)


def holder_order(key):
    return jax.random.permutation(jax.random.fold_in(key, 7), ADAPTER_SLOTS).astype(jnp.int32)


def draw_plain_query_rows(key, part):
    query_draw = query_noise(key)
    return query_draw.astype(jnp.bfloat16)


def draw_cached_key_rows(key, part):
    key = jax.random.fold_in(key, 11)
    first_key = jax.random.fold_in(key, 0)
    keys_drawn = jax.random.truncated_normal(first_key, -4.0, 4.0, (ROWS, KV_HEADS, CACHE, HEAD_DIM), jnp.float32)
    return keys_drawn.astype(jnp.bfloat16)


def draw_live_cache_length(key, part):
    key = jax.random.fold_in(key, 21)
    first_key, second_key = jax.random.split(key)
    lengths = jax.random.randint(first_key, (ROWS,), 2, CACHE + 1).astype(jnp.int32)
    blocks = ROWS // ROW_DEV
    position = jax.random.randint(second_key, (blocks,), 0, ROW_DEV).astype(jnp.int32)
    full_rows = jnp.arange(blocks, dtype=jnp.int32) * ROW_DEV + position
    return lengths.at[full_rows].set(CACHE).astype(jnp.int32)


def draw_slot_of_adapter(key, part):
    held_at = holder_order(key)
    return jnp.argsort(held_at).astype(jnp.int32)


def draw_tenant(key, part):
    held_at = holder_order(key)
    key = jax.random.fold_in(key, 31)
    hot_key, level_key, noise_key, shuffle_key = jax.random.split(key, 4)
    blocks = ROWS // ROW_DEV
    candidates = ADAPTER_SLOTS * CAP
    hottest = jax.random.randint(hot_key, (), 0, ADAPTER_SLOTS).astype(jnp.int32)
    levels = jax.random.randint(level_key, (ADAPTER_SLOTS,), 0, 4).astype(jnp.int32)
    counter = jnp.arange(candidates, dtype=jnp.int32)
    owner_of = counter // CAP
    noise_int = jax.random.randint(noise_key, (blocks, candidates), 0, 1024).astype(jnp.int32)
    scores = (noise_int + 256 * levels[owner_of][None, :]) * candidates + counter[None, :]
    scores = jnp.where((owner_of == hottest)[None, :], -1 - counter[None, :], scores)
    selected_weights = lax.top_k(scores, ROW_DEV - CAP)[1] // CAP
    owners = jnp.concatenate([jnp.full((blocks, CAP), hottest, jnp.int32), selected_weights.astype(jnp.int32)], axis=1)
    shuffle_int = jax.random.randint(shuffle_key, (blocks, ROW_DEV), 0, 1 << 20).astype(jnp.int32) * ROW_DEV + jnp.arange(ROW_DEV, dtype=jnp.int32)[None, :]
    shuffled_order = jnp.argsort(shuffle_int, axis=1)
    mixed_owners = jnp.take_along_axis(owners, shuffled_order, axis=1)
    return held_at[mixed_owners.reshape(ROWS)].astype(jnp.int32)


def block_levels(key, dims, cuts, least, largest):
    gain = 1.0
    for dim, blocks in cuts:
        steps = jax.random.uniform(jax.random.fold_in(jax.random.fold_in(key, 6), dim), (blocks,), jnp.float32, least / len(cuts), largest / len(cuts))
        gain = gain * jnp.repeat(jnp.exp(steps), dims[dim] // blocks).reshape((-1,) + (1,) * (len(dims) - 1 - dim))
    return gain


def gaussian(key, dims, scale, reach, cuts=(), kind=jnp.bfloat16):
    result = jax.random.normal(key, dims, jnp.float32) * scale
    if len(cuts) > 0:
        result = block_levels(key, dims, cuts, -0.22, 0.18) * result
    return jnp.clip(result, min=-reach, max=reach).astype(kind)


def setup_inputs(seed: int = 0, part: int = 0) -> dict:
    key_of = jax.random.split(jax.random.key(seed), 15)
    part_splits = jax.random.split(jax.random.fold_in(key_of[14], part), 15)
    return {
        "normed_layer_input": gaussian(part_splits[0], (ROWS, MODEL_WIDTH), 1.0, 6.0, ((0, 8),)),
        "plain_query_rows": draw_plain_query_rows(jax.random.fold_in(jax.random.fold_in(key_of[14], part), 71), part),
        "plain_key_rows": gaussian(part_splits[2], (ROWS, KEY_FEATURES), 1.0, 6.0, ((0, 8), (1, 2))),
        "plain_value_rows": gaussian(part_splits[3], (ROWS, KEY_FEATURES), 1.0, 6.0, ((0, 8), (1, 2))),
        "cached_key_rows": draw_cached_key_rows(jax.random.fold_in(jax.random.fold_in(key_of[14], part), 71), part),
        "cached_value_rows": gaussian(part_splits[5], (ROWS, KV_HEADS, CACHE, HEAD_DIM), 1.0, 6.0, ((0, 8), (1, 2))),
        "live_cache_length": draw_live_cache_length(jax.random.fold_in(jax.random.fold_in(key_of[14], part), 71), part),
        "tenant": draw_tenant(jax.random.fold_in(jax.random.fold_in(key_of[14], part), 71), part),
        "slot_of_adapter": draw_slot_of_adapter(jax.random.fold_in(jax.random.fold_in(key_of[14], part), 71), part),
        "stacked_down_weight": gaussian(key_of[9], (ADAPTER_SLOTS, 3 * ADAPTER_RANK, MODEL_WIDTH), MODEL_WIDTH ** -0.5, 0.0625, ((0, 8),)),
        "query_up_weight": gaussian(key_of[10], (ADAPTER_SLOTS, ADAPTER_RANK, MODEL_WIDTH), ADAPTER_RANK ** -0.5, 0.75, ((0, 8), (2, 2))),
        "key_value_up_weight": gaussian(key_of[11], (ADAPTER_SLOTS, 2, ADAPTER_RANK, KEY_FEATURES), ADAPTER_RANK ** -0.5, 0.75, ((0, 8), (3, 2))),
        "output_down_weight": gaussian(key_of[12], (ADAPTER_SLOTS, ADAPTER_RANK, MODEL_WIDTH), (MODEL_WIDTH // 32) ** -0.5, 0.375, ((0, 8), (2, 2))),
        "output_up_weight": gaussian(key_of[13], (ADAPTER_SLOTS, ADAPTER_RANK, MODEL_WIDTH), ADAPTER_RANK ** -0.5, 0.75, ((0, 8), (2, 2))),
    }


ADAPTER_SCALE = 0.5


def reference(normed_layer_input, plain_query_rows, plain_key_rows, plain_value_rows, cached_key_rows, cached_value_rows, live_cache_length, tenant, slot_of_adapter, stacked_down_weight, query_up_weight, key_value_up_weight, output_down_weight, output_up_weight):
    holder = slot_of_adapter[tenant].astype(jnp.int32)
    per_slot = N_WIDE * CAP
    one_hot = (holder[:, None] == jnp.arange(ADAPTER_SLOTS, dtype=jnp.int32)[None, :]).astype(jnp.int32)
    before = (jnp.cumsum(one_hot, axis=0) - one_hot).astype(jnp.int32)
    order_in = jnp.sum(before * one_hot, axis=1).astype(jnp.int32)
    flat_slot = (holder * per_slot + order_in).astype(jnp.int32)
    row_table = jnp.full((ADAPTER_SLOTS * per_slot,), ROWS, jnp.int32).at[flat_slot].set(jnp.arange(ROWS, dtype=jnp.int32))
    row_table = row_table.reshape(ADAPTER_SLOTS, per_slot)

    def adapter_projected(rows_in, compute):
        padded = jnp.concatenate([rows_in, jnp.zeros((1, rows_in.shape[1]), rows_in.dtype)], axis=0)

        def one_slot(slot_index):
            selected_weights = padded[row_table[slot_index]]
            return compute(selected_weights, slot_index)

        outputs = lax.map(one_slot, jnp.arange(ADAPTER_SLOTS, dtype=jnp.int32))
        flattened = outputs.reshape(ADAPTER_SLOTS * per_slot, outputs.shape[2])
        return flattened[flat_slot]

    def qkv_deltas(selected_weights, slot_index):
        stacked_rank_rows = jnp.dot(selected_weights, stacked_down_weight[slot_index].T, preferred_element_type=jnp.float32).astype(jnp.bfloat16)
        query_correction = jnp.dot(stacked_rank_rows[:, :ADAPTER_RANK], query_up_weight[slot_index], preferred_element_type=jnp.float32).astype(jnp.bfloat16)
        key_correction = jnp.dot(stacked_rank_rows[:, ADAPTER_RANK:2 * ADAPTER_RANK], key_value_up_weight[slot_index, 0], preferred_element_type=jnp.float32).astype(jnp.bfloat16)
        value_correction = jnp.dot(stacked_rank_rows[:, 2 * ADAPTER_RANK:], key_value_up_weight[slot_index, 1], preferred_element_type=jnp.float32).astype(jnp.bfloat16)
        return jnp.concatenate([query_correction, key_correction, value_correction], axis=1)

    corrections = adapter_projected(normed_layer_input, qkv_deltas)
    query_matrix = (plain_query_rows.astype(jnp.float32) + ADAPTER_SCALE * corrections[:, :MODEL_WIDTH].astype(jnp.float32)).astype(jnp.bfloat16)
    fresh_key = (plain_key_rows.astype(jnp.float32) + ADAPTER_SCALE * corrections[:, MODEL_WIDTH:MODEL_WIDTH + KEY_FEATURES].astype(jnp.float32)).astype(jnp.bfloat16)
    fresh_value = (plain_value_rows.astype(jnp.float32) + ADAPTER_SCALE * corrections[:, MODEL_WIDTH + KEY_FEATURES:].astype(jnp.float32)).astype(jnp.bfloat16)
    group_size = HEADS // KV_HEADS
    inverse_root = HEAD_DIM ** -0.5

    def attend(block_id):
        start_row = (block_id * ROW_DEV).astype(jnp.int32)
        q_block = lax.dynamic_slice_in_dim(query_matrix, start_row, ROW_DEV).reshape(ROW_DEV, KV_HEADS, group_size, HEAD_DIM).astype(jnp.float32)
        key_block = lax.dynamic_slice_in_dim(cached_key_rows, start_row, ROW_DEV).astype(jnp.float32)
        value_block = lax.dynamic_slice_in_dim(cached_value_rows, start_row, ROW_DEV).astype(jnp.float32)
        own_key = lax.dynamic_slice_in_dim(fresh_key, start_row, ROW_DEV).reshape(ROW_DEV, KV_HEADS, HEAD_DIM).astype(jnp.float32)
        own_value = lax.dynamic_slice_in_dim(fresh_value, start_row, ROW_DEV).reshape(ROW_DEV, KV_HEADS, 1, HEAD_DIM).astype(jnp.float32)
        lengths = lax.dynamic_slice_in_dim(live_cache_length, start_row, ROW_DEV)
        cache_scores = jnp.einsum("rgqd,rgcd->rgqc", q_block, key_block) * inverse_root
        own_scores = jnp.einsum("rgqd,rgd->rgq", q_block, own_key) * inverse_root
        valid_cache = jnp.arange(CACHE, dtype=jnp.int32)[None, :] < lengths[:, None]
        cache_scores = jnp.where(valid_cache[:, None, None, :], cache_scores, -jnp.inf)
        highest = jnp.maximum(jnp.max(cache_scores, axis=-1), own_scores)
        cache_exp = jnp.exp(cache_scores - highest[..., None])
        own_exp = jnp.exp(own_scores - highest)
        denominator = jnp.sum(cache_exp, axis=-1) + own_exp
        cache_weight = (cache_exp / denominator[..., None]).astype(jnp.bfloat16).astype(jnp.float32)
        own_weight = (own_exp / denominator).astype(jnp.bfloat16).astype(jnp.float32)
        attended = jnp.einsum("rgqc,rgcd->rgqd", cache_weight, value_block) + own_weight[..., None] * own_value
        return attended.reshape(ROW_DEV, MODEL_WIDTH).astype(jnp.bfloat16)

    context = lax.map(attend, jnp.arange(N_WIDE, dtype=jnp.int32)).reshape(ROWS, MODEL_WIDTH)

    def output_correction(selected_weights, slot_index):
        output_rank_rows = jnp.dot(selected_weights, output_down_weight[slot_index].T, preferred_element_type=jnp.float32).astype(jnp.bfloat16)
        return (ADAPTER_SCALE * jnp.dot(output_rank_rows, output_up_weight[slot_index], preferred_element_type=jnp.float32)).astype(jnp.bfloat16)

    adapter_output_term = adapter_projected(context, output_correction)
    return context, adapter_output_term
```

```python
import functools

import jax
import jax.numpy as jnp
from jax import lax
from jax.experimental import pallas as pl
from jax.experimental.pallas import tpu as pltpu
from jax.sharding import PartitionSpec as P

ADAPTER_SCALE = 0.5
CHUNKS = 2
F32 = jnp.float32
BF16 = jnp.bfloat16
VMEM = pl.BlockSpec(memory_space=pltpu.VMEM)
SMEM = pl.BlockSpec(memory_space=pltpu.SMEM)


def call(body, out_shape, in_specs, out_specs=None, scratch=(), flops=0, moved=0, limit=24):
    return pl.pallas_call(
        body,
        out_shape=out_shape,
        in_specs=in_specs,
        out_specs=jax.tree.map(lambda _: VMEM, out_shape) if out_specs is None else out_specs,
        scratch_shapes=scratch,
        cost_estimate=pl.CostEstimate(flops=flops, bytes_accessed=moved, transcendentals=0),
        compiler_params=pltpu.CompilerParams(vmem_limit_bytes=limit * 1024 * 1024),
    )


def iota(shape, dim):
    return lax.broadcasted_iota(jnp.int32, shape, dim)


def dot(a, b):
    return lax.dot_general(a, b, (((1,), (0,)), ((), ())), preferred_element_type=F32)


def dot_t(a, b):
    return lax.dot_general(a, b, (((1,), (1,)), ((), ())), preferred_element_type=F32)


def scalars_to_row(read, rows):
    lane = iota((1, rows), 1)
    row = jnp.zeros((1, rows), jnp.int32)
    for r in range(rows):
        row = jnp.where(lane == r, read(r), row)
    return row


def pack_body(capacity, tenant_ref, slot_ref, x_ref, dest_ref, packed_ref, count_ref):
    rows = x_ref.shape[0]
    slots, width = packed_ref.shape
    first = lax.axis_index("wide") * rows
    for d in range(slots // capacity):
        count_ref[d] = 0
    for r in range(rows):
        holder = slot_ref[tenant_ref[first + r]]
        place = count_ref[holder]
        count_ref[holder] = place + 1
        dest_ref[r] = holder * capacity + place
    dest = scalars_to_row(lambda r: dest_ref[r], rows)
    chosen = (iota((slots, rows), 0) == dest).astype(F32).astype(BF16)
    start = pl.multiple_of(lax.axis_index("tp") * width, width)
    packed_ref[...] = dot(chosen, x_ref[:, pl.ds(start, width)]).astype(BF16)


def prep_body(
    group, dest_ref, len_ref, pq_ref, pk_ref, pv_ref,
    pqt_ref, pkt_ref, pvt_ref, spread_ref, take_ref, place_ref, home_ref, bias_ref,
):
    rows, kv_width = pk_ref.shape
    head_dim = pqt_ref.shape[2]
    kv_heads = pqt_ref.shape[0]
    lines = rows * group
    slots = home_ref.shape[1]
    shift = group.bit_length() - 1
    dest_row = scalars_to_row(lambda r: dest_ref[r], rows)
    len_row = scalars_to_row(lambda r: len_ref[r], rows)
    mine = (iota((lines, rows), 0) >> shift) == iota((lines, rows), 1)
    dest_line = jnp.sum(jnp.where(mine, dest_row, 0), axis=1, keepdims=True)
    len_line = jnp.sum(jnp.where(mine, len_row, 0), axis=1, keepdims=True)
    head_line = iota((lines, 1), 0) & (group - 1)
    row_line = iota((lines, 1), 0) >> shift
    to_line = (iota((lines, group * rows), 1) == head_line * rows + row_line).astype(F32).astype(BF16)
    repeat = mine.astype(F32).astype(BF16)
    for g in range(kv_heads):
        stacked = jnp.concatenate(
            [pq_ref[:, (g * group + h) * head_dim : (g * group + h + 1) * head_dim] for h in range(group)], axis=0
        )
        pqt_ref[g] = dot(to_line, stacked).astype(BF16)
        pkt_ref[g] = dot(repeat, pk_ref[:, g * head_dim : (g + 1) * head_dim]).astype(BF16)
        pvt_ref[g] = dot(repeat, pv_ref[:, g * head_dim : (g + 1) * head_dim]).astype(BF16)
    spread_ref[...] = jnp.where(
        iota((lines, group * slots), 1) == head_line * slots + dest_line, ADAPTER_SCALE, 0.0
    ).astype(BF16)
    take_ref[...] = jnp.where(iota((lines, slots), 1) == dest_line, ADAPTER_SCALE, 0.0).astype(BF16)
    here = iota((rows, lines), 0) == (iota((rows, lines), 1) >> shift)
    eye = iota((rows, rows), 0) == iota((rows, rows), 1)
    dest_col = jnp.sum(jnp.where(eye, dest_row, 0), axis=1, keepdims=True)
    dest_lane = jnp.sum(jnp.where(here, dest_col, 0), axis=0, keepdims=True)
    head_lane = iota((1, lines), 1) & (group - 1)
    row_lane = iota((1, lines), 1) >> shift
    place_ref[: group * slots] = (
        (iota((group * slots, lines), 0) == head_lane * slots + dest_lane).astype(F32).astype(BF16)
    )
    place_ref[group * slots :] = (
        (iota((group * rows, lines), 0) == head_lane * rows + row_lane).astype(F32).astype(BF16)
    )
    home_ref[...] = (iota((rows, slots), 1) == dest_col).astype(F32).astype(BF16)
    bias_ref[...] = jnp.where(iota(bias_ref.shape, 1) < len_line, 0.0, -jnp.inf)


def up_body(group, mine_ref, other_ref, uq_ref, ukv_ref, *out_refs):
    rank = uq_ref.shape[1]
    total = (mine_ref[...] + other_ref[...]).astype(BF16)
    kv_width = ukv_ref.shape[3]
    width = kv_width // len(out_refs)
    q_width = width * group
    for c, out_ref in enumerate(out_refs):
        out_ref[:, :q_width] = dot(
            total[:, :rank], uq_ref[0, :, c * q_width : (c + 1) * q_width]
        ).astype(BF16)
        for i in range(2):
            out_ref[:, q_width + i * width : q_width + (i + 1) * width] = dot(
                total[:, (i + 1) * rank : (i + 2) * rank], ukv_ref[0, i, :, c * width : (c + 1) * width]
            ).astype(BF16)


def attend_body(
    first_head, heads, group, ret_ref, pqt_ref, pkt_ref, pvt_ref, k_ref, v_ref,
    spread_ref, take_ref, place_ref, bias_ref, packed_ref, context_ref,
):
    rows = context_ref.shape[0]
    slots = packed_ref.shape[0]
    head_dim = pqt_ref.shape[2]
    scale = head_dim ** (-0.5)
    spread, take, place = spread_ref[...], take_ref[...], place_ref[...]
    bias = bias_ref[...]
    k_base = heads * group * head_dim
    v_base = k_base + heads * head_dim
    for i in range(heads):
        g = first_head + i
        stacked = jnp.concatenate(
            [ret_ref[:, (i * group + h) * head_dim : (i * group + h + 1) * head_dim] for h in range(group)], axis=0
        )
        query = (pqt_ref[g].astype(F32) + dot(spread, stacked)).astype(BF16).astype(F32)
        new_key = (
            pkt_ref[g].astype(F32) + dot(take, ret_ref[:, k_base + i * head_dim : k_base + (i + 1) * head_dim])
        ).astype(BF16).astype(F32)
        new_value = (
            pvt_ref[g].astype(F32) + dot(take, ret_ref[:, v_base + i * head_dim : v_base + (i + 1) * head_dim])
        ).astype(BF16).astype(F32)
        own = jnp.sum(query * new_key, axis=1, keepdims=True) * scale
        score = jnp.concatenate(
            [dot_t(query[r * group : (r + 1) * group].astype(BF16), k_ref[r, g]) for r in range(rows)], axis=0
        )
        score = score * scale + bias
        highest = jnp.maximum(jnp.max(score, axis=1, keepdims=True), own)
        raised = jnp.exp(score - highest)
        own_raised = jnp.exp(own - highest)
        inverse = 1.0 / (jnp.sum(raised, axis=1, keepdims=True) + own_raised)
        weight = raised * inverse
        own_weight = (own_raised * inverse).astype(BF16).astype(F32)
        attended = jnp.concatenate(
            [dot(weight[r * group : (r + 1) * group].astype(BF16), v_ref[r, g]) for r in range(rows)], axis=0
        )
        context = (attended + own_weight * new_value).astype(BF16)
        laid = dot(place, context).astype(BF16)
        for h in range(group):
            columns = slice((i * group + h) * head_dim, (i * group + h + 1) * head_dim)
            packed_ref[:, columns] = laid[h * slots : (h + 1) * slots]
            base = group * slots + h * rows
            context_ref[:, columns] = laid[base : base + rows]


def output_up_body(mine_ref, other_ref, uo_ref, out_ref):
    total = (mine_ref[...] + other_ref[...]).astype(BF16)
    out_ref[...] = (ADAPTER_SCALE * dot(total, uo_ref[0])).astype(BF16)


def unpack_body(home_ref, ret_ref, out_ref):
    out_ref[...] = dot(home_ref[...], ret_ref[...]).astype(BF16)


def exchange(rows, wide_count):
    slots, width = rows.shape
    moved = lax.all_to_all(
        rows.reshape(wide_count, slots // wide_count, width), "wide", split_axis=0, concat_axis=0, tiled=True
    )
    return moved.reshape(slots, width)


def other_core(value):
    return lax.ppermute(value, "tp", [(0, 1), (1, 0)])


def shards(
    normed_layer_input,
    plain_query_rows,
    plain_key_rows,
    plain_value_rows,
    cached_key_rows,
    cached_value_rows,
    live_cache_length,
    tenant,
    slot_of_adapter,
    stacked_down_weight,
    query_up_weight,
    key_value_up_weight,
    output_down_weight,
    output_up_weight,
):
    wide_count = lax.axis_size("wide")
    rows, features = normed_layer_input.shape
    half = features // lax.axis_size("tp")
    capacity = max(2, 2 * rows // wide_count)
    slots = wide_count * capacity
    kv_heads, cache_size, head_dim = cached_key_rows.shape[1:]
    query_width = plain_query_rows.shape[1]
    group = query_width // head_dim // kv_heads
    lines = rows * group
    struct = jax.ShapeDtypeStruct

    dest, packed = call(
        functools.partial(pack_body, capacity),
        (struct((rows,), jnp.int32), struct((slots, half), BF16)),
        [SMEM, SMEM, VMEM],
        (SMEM, VMEM),
        scratch=[pltpu.SMEM((wide_count,), jnp.int32)],
        moved=4 * slots * half,
    )(tenant, slot_of_adapter, normed_layer_input)
    received = exchange(packed, wide_count)

    pqt, pkt, pvt, spread, take, place, home, bias = call(
        functools.partial(prep_body, group),
        (
            struct((kv_heads, lines, head_dim), BF16),
            struct((kv_heads, lines, head_dim), BF16),
            struct((kv_heads, lines, head_dim), BF16),
            struct((lines, group * slots), BF16),
            struct((lines, slots), BF16),
            struct((group * (slots + rows), lines), BF16),
            struct((rows, slots), BF16),
            struct((lines, cache_size), F32),
        ),
        [SMEM, SMEM, VMEM, VMEM, VMEM],
        moved=6000000,
    )(dest, live_cache_length, plain_query_rows, plain_key_rows, plain_value_rows)

    down_here = lax.dynamic_slice_in_dim(stacked_down_weight[0], lax.axis_index("tp") * half, half, axis=1)
    rank_part = dot_t(received, down_here)
    width = kv_heads // CHUNKS
    terms = call(
        functools.partial(up_body, group),
        tuple(struct((slots, width * (group + 2) * head_dim), BF16) for _ in range(CHUNKS)),
        [VMEM] * 4,
        moved=2000000,
    )(rank_part, other_core(rank_part), query_up_weight, key_value_up_weight)
    returned = [exchange(term, wide_count) for term in terms]
    contexts = []
    rank_o = None
    for c in range(CHUNKS):
        chunk_width = width * group * head_dim
        outgoing, context = call(
            functools.partial(attend_body, c * width, width, group),
            (struct((slots, chunk_width), BF16), struct((rows, chunk_width), BF16)),
            [VMEM] * 10,
            moved=8000000,
            limit=32,
        )(returned[c], pqt, pkt, pvt, cached_key_rows, cached_value_rows, spread, take, place, bias)
        contexts.append(context)
        arrived = exchange(outgoing, wide_count)
        part = dot_t(arrived, output_down_weight[0][:, c * chunk_width : (c + 1) * chunk_width])
        rank_o = part if rank_o is None else rank_o + part
    out_terms = call(
        output_up_body, struct((slots, query_width), BF16), [VMEM] * 3, moved=1200000
    )(rank_o, other_core(rank_o), output_up_weight)
    adapter_output_term = call(
        unpack_body, struct((rows, query_width), BF16), [VMEM] * 2, moved=1000000
    )(home, exchange(out_terms, wide_count))
    return jnp.concatenate(contexts, axis=1), adapter_output_term


def solution(mesh):
    return jax.shard_map(
        shards,
        mesh=mesh,
        in_specs=(
            P(("groups", "wide"), None),
            P(("groups", "wide"), "tp"),
            P(("groups", "wide"), "tp"),
            P(("groups", "wide"), "tp"),
            P(("groups", "wide"), "tp", None, None),
            P(("groups", "wide"), "tp", None, None),
            P(("groups", "wide")),
            P("groups"),
            P("groups"),
            P("wide", None, None),
            P("wide", None, "tp"),
            P("wide", None, None, "tp"),
            P("wide", None, "tp"),
            P("wide", None, "tp"),
        ),
        out_specs=(P(("groups", "wide"), "tp"), P(("groups", "wide"), "tp")),
        check_vma=False,
    )
```

```python
import functools

import jax
import jax.numpy as jnp
from jax import lax
from jax.experimental import pallas as pl
from jax.experimental.pallas import tpu as pltpu
from jax.sharding import PartitionSpec as P

ADAPTER_SCALE = 0.5
F32 = jnp.float32
BF16 = jnp.bfloat16
VMEM = pl.BlockSpec(memory_space=pltpu.VMEM)
SMEM = pl.BlockSpec(memory_space=pltpu.SMEM)
HBM = pl.BlockSpec(memory_space=pltpu.HBM)
DMA = pltpu.SemaphoreType.DMA


def call(body, out_shape, in_specs, out_specs=None, scratch=(), flops=0, moved=0, limit=58):
    return pl.pallas_call(
        body,
        out_shape=out_shape,
        in_specs=in_specs,
        out_specs=jax.tree.map(lambda _: VMEM, out_shape) if out_specs is None else out_specs,
        scratch_shapes=scratch,
        cost_estimate=pl.CostEstimate(flops=flops, bytes_accessed=moved, transcendentals=0),
        compiler_params=pltpu.CompilerParams(vmem_limit_bytes=limit * 1024 * 1024),
    )


def iota(shape, dim):
    return lax.broadcasted_iota(jnp.int32, shape, dim)


def dot(a, b):
    return lax.dot_general(a, b, (((1,), (0,)), ((), ())), preferred_element_type=F32)


def dot_t(a, b):
    return lax.dot_general(a, b, (((1,), (1,)), ((), ())), preferred_element_type=F32)


def scalars_to_row(read, rows):
    lane = iota((1, rows), 1)
    row = jnp.zeros((1, rows), jnp.int32)
    for r in range(rows):
        row = jnp.where(lane == r, read(r), row)
    return row


def pack_body(
    capacity, tenant_hbm, slot_hbm, x_hbm, dest_ref, packed_ref, tenant_ref, slot_ref, count_ref, x_ref, sems
):
    slots, width = packed_ref.shape
    rows = x_ref.shape[0]
    start = pl.multiple_of(lax.axis_index("tp") * width, width)
    copies = [
        pltpu.make_async_copy(tenant_hbm, tenant_ref, sems.at[0]),
        pltpu.make_async_copy(slot_hbm, slot_ref, sems.at[1]),
        pltpu.make_async_copy(x_hbm.at[:, pl.ds(start, width)], x_ref, sems.at[2]),
    ]
    for copy in copies:
        copy.start()
    for d in range(slots // capacity):
        count_ref[d] = 0
    copies[0].wait()
    copies[1].wait()
    first = lax.axis_index("wide") * rows
    lane = iota((1, rows), 1)
    dest = jnp.zeros((1, rows), jnp.int32)
    for r in range(rows):
        holder = slot_ref[tenant_ref[first + r]]
        place = count_ref[holder]
        count_ref[holder] = place + 1
        slot = holder * capacity + place
        dest_ref[r] = slot
        dest = jnp.where(lane == r, slot, dest)
    chosen = (iota((slots, rows), 0) == dest).astype(F32).astype(BF16)
    copies[2].wait()
    packed_ref[...] = dot(chosen, x_ref[...]).astype(BF16)


def prep_body(
    group, dest_ref, len_ref, pq_hbm, pk_hbm, pv_hbm, *refs
):
    outs, refs = refs[:8], refs[8:]
    pqt_ref, pkt_ref, pvt_ref, spread_ref, take_ref, place_ref, home_ref, bias_ref = refs[:8]
    pq_ref, pk_ref, pv_ref, sems = refs[8:]
    plain = [
        pltpu.make_async_copy(source, target, sems.at[i])
        for i, (source, target) in enumerate(((pq_hbm, pq_ref), (pk_hbm, pk_ref), (pv_hbm, pv_ref)))
    ]
    for copy in plain:
        copy.start()
    rows = pk_ref.shape[0]
    head_dim = pqt_ref.shape[2]
    kv_heads = pqt_ref.shape[0]
    lines = rows * group
    slots = home_ref.shape[1]
    shift = group.bit_length() - 1
    dest_row = scalars_to_row(lambda r: dest_ref[r], rows)
    len_row = scalars_to_row(lambda r: len_ref[r], rows)
    mine = (iota((lines, rows), 0) >> shift) == iota((lines, rows), 1)
    dest_line = jnp.sum(jnp.where(mine, dest_row, 0), axis=1, keepdims=True)
    len_line = jnp.sum(jnp.where(mine, len_row, 0), axis=1, keepdims=True)
    head_line = iota((lines, 1), 0) & (group - 1)
    row_line = iota((lines, 1), 0) >> shift
    to_line = (iota((lines, group * rows), 1) == head_line * rows + row_line).astype(F32).astype(BF16)
    repeat = mine.astype(F32).astype(BF16)
    for copy in plain:
        copy.wait()
    for g in range(kv_heads):
        stacked = jnp.concatenate(
            [pq_ref[:, (g * group + h) * head_dim : (g * group + h + 1) * head_dim] for h in range(group)], axis=0
        )
        pqt_ref[g] = dot(to_line, stacked).astype(BF16)
        pkt_ref[g] = dot(repeat, pk_ref[:, g * head_dim : (g + 1) * head_dim]).astype(BF16)
        pvt_ref[g] = dot(repeat, pv_ref[:, g * head_dim : (g + 1) * head_dim]).astype(BF16)
    spread_ref[...] = jnp.where(
        iota((lines, group * slots), 1) == head_line * slots + dest_line, ADAPTER_SCALE, 0.0
    ).astype(BF16)
    take_ref[...] = jnp.where(iota((lines, slots), 1) == dest_line, ADAPTER_SCALE, 0.0).astype(BF16)
    here = iota((rows, lines), 0) == (iota((rows, lines), 1) >> shift)
    eye = iota((rows, rows), 0) == iota((rows, rows), 1)
    dest_col = jnp.sum(jnp.where(eye, dest_row, 0), axis=1, keepdims=True)
    dest_lane = jnp.sum(jnp.where(here, dest_col, 0), axis=0, keepdims=True)
    head_lane = iota((1, lines), 1) & (group - 1)
    row_lane = iota((1, lines), 1) >> shift
    place_ref[: group * slots] = (
        (iota((group * slots, lines), 0) == head_lane * slots + dest_lane).astype(F32).astype(BF16)
    )
    place_ref[group * slots :] = (
        (iota((group * rows, lines), 0) == head_lane * rows + row_lane).astype(F32).astype(BF16)
    )
    home_ref[...] = (iota((rows, slots), 1) == dest_col).astype(F32).astype(BF16)
    bias_ref[...] = jnp.where(iota(bias_ref.shape, 1) < len_line, 0.0, -jnp.inf)
    kept = [pltpu.make_async_copy(refs[i], outs[i], sems.at[3 + i]) for i in range(8)]
    for copy in kept:
        copy.start()
    for copy in kept:
        copy.wait()


def up_body(group, mine_ref, other_ref, uq_ref, ukv_ref, out_ref):
    rank = uq_ref.shape[1]
    total = (mine_ref[...] + other_ref[...]).astype(BF16)
    q_width = uq_ref.shape[2]
    width = ukv_ref.shape[3]
    out_ref[:, :q_width] = dot(total[:, :rank], uq_ref[0]).astype(BF16)
    for i in range(2):
        out_ref[:, q_width + i * width : q_width + (i + 1) * width] = dot(
            total[:, (i + 1) * rank : (i + 2) * rank], ukv_ref[0, i]
        ).astype(BF16)


def attend_body(
    group, ret_ref, k_hbm, v_hbm, pqt_hbm, pkt_hbm, pvt_hbm, spread_hbm, take_hbm, place_hbm, bias_hbm,
    packed_ref, context_ref,
    pqt_ref, pkt_ref, pvt_ref, spread_ref, take_ref, place_ref, bias_ref, k_buf, v_buf, sems,
):
    heads, rows = k_buf.shape[:2]
    slots = packed_ref.shape[0]
    head_dim = pqt_ref.shape[2]
    pairs = [
        (spread_hbm, spread_ref), (pqt_hbm, pqt_ref), (take_hbm, take_ref), (pkt_hbm, pkt_ref),
        (pvt_hbm, pvt_ref), (bias_hbm, bias_ref), (place_hbm, place_ref),
    ]
    prepared = [pltpu.make_async_copy(a, b, sems.at[i]) for i, (a, b) in enumerate(pairs)]
    cached = [
        [
            pltpu.make_async_copy(source.at[:, g], target.at[g], sems.at[len(pairs) + 2 * g + j])
            for j, (source, target) in enumerate(((k_hbm, k_buf), (v_hbm, v_buf)))
        ]
        for g in range(heads)
    ]
    for copy in prepared[:6] + cached[0] + prepared[6:]:
        copy.start()
    for g in range(1, heads):
        for copy in cached[g]:
            copy.start()
    for copy in prepared:
        copy.wait()
    scale = head_dim ** (-0.5)
    spread, take, place = spread_ref[...], take_ref[...], place_ref[...]
    bias = bias_ref[...]
    k_base = heads * group * head_dim
    v_base = k_base + heads * head_dim
    for i in range(heads):
        g = i
        stacked = jnp.concatenate(
            [ret_ref[:, (i * group + h) * head_dim : (i * group + h + 1) * head_dim] for h in range(group)], axis=0
        )
        query = (pqt_ref[g].astype(F32) + dot(spread, stacked)).astype(BF16).astype(F32)
        new_key = (
            pkt_ref[g].astype(F32) + dot(take, ret_ref[:, k_base + i * head_dim : k_base + (i + 1) * head_dim])
        ).astype(BF16).astype(F32)
        new_value = (
            pvt_ref[g].astype(F32) + dot(take, ret_ref[:, v_base + i * head_dim : v_base + (i + 1) * head_dim])
        ).astype(BF16).astype(F32)
        own = jnp.sum(query * new_key, axis=1, keepdims=True) * scale
        cached[g][0].wait()
        score = jnp.concatenate(
            [dot_t(query[r * group : (r + 1) * group].astype(BF16), k_buf[g, r]) for r in range(rows)], axis=0
        )
        score = score * scale + bias
        highest = jnp.maximum(jnp.max(score, axis=1, keepdims=True), own)
        raised = jnp.exp(score - highest)
        own_raised = jnp.exp(own - highest)
        inverse = 1.0 / (jnp.sum(raised, axis=1, keepdims=True) + own_raised)
        weight = raised * inverse
        own_weight = (own_raised * inverse).astype(BF16).astype(F32)
        cached[g][1].wait()
        attended = jnp.concatenate(
            [dot(weight[r * group : (r + 1) * group].astype(BF16), v_buf[g, r]) for r in range(rows)], axis=0
        )
        context = (attended + own_weight * new_value).astype(BF16)
        laid = dot(place, context).astype(BF16)
        for h in range(group):
            columns = slice((i * group + h) * head_dim, (i * group + h + 1) * head_dim)
            packed_ref[:, columns] = laid[h * slots : (h + 1) * slots]
            base = group * slots + h * rows
            context_ref[:, columns] = laid[base : base + rows]


def output_up_body(mine_ref, other_ref, uo_ref, out_ref):
    total = (mine_ref[...] + other_ref[...]).astype(BF16)
    out_ref[...] = (ADAPTER_SCALE * dot(total, uo_ref[0])).astype(BF16)


def unpack_body(home_ref, ret_ref, out_ref):
    out_ref[...] = dot(home_ref[...], ret_ref[...]).astype(BF16)


def exchange(rows, wide_count):
    slots, width = rows.shape
    moved = lax.all_to_all(
        rows.reshape(wide_count, slots // wide_count, width), "wide", split_axis=0, concat_axis=0, tiled=True
    )
    return moved.reshape(slots, width)


def other_core(value):
    return lax.ppermute(value, "tp", [(0, 1), (1, 0)])


def shards(
    normed_layer_input,
    plain_query_rows,
    plain_key_rows,
    plain_value_rows,
    cached_key_rows,
    cached_value_rows,
    live_cache_length,
    tenant,
    slot_of_adapter,
    stacked_down_weight,
    query_up_weight,
    key_value_up_weight,
    output_down_weight,
    output_up_weight,
):
    wide_count = lax.axis_size("wide")
    rows, features = normed_layer_input.shape
    half = features // lax.axis_size("tp")
    capacity = max(2, 2 * rows // wide_count)
    slots = wide_count * capacity
    kv_heads, cache_size, head_dim = cached_key_rows.shape[1:]
    query_width = plain_query_rows.shape[1]
    group = query_width // head_dim // kv_heads
    lines = rows * group
    struct = jax.ShapeDtypeStruct

    dest, packed = call(
        functools.partial(pack_body, capacity),
        (struct((rows,), jnp.int32), struct((slots, half), BF16)),
        [HBM, HBM, HBM],
        (SMEM, VMEM),
        scratch=[
            pltpu.SMEM(tenant.shape, jnp.int32),
            pltpu.SMEM(slot_of_adapter.shape, jnp.int32),
            pltpu.SMEM((wide_count,), jnp.int32),
            pltpu.VMEM((rows, half), BF16),
            DMA((3,)),
        ],
        moved=4 * slots * half,
    )(tenant, slot_of_adapter, normed_layer_input)
    received = exchange(packed, wide_count)

    prepared = (
        struct((kv_heads, lines, head_dim), BF16),
        struct((kv_heads, lines, head_dim), BF16),
        struct((kv_heads, lines, head_dim), BF16),
        struct((lines, group * slots), BF16),
        struct((lines, slots), BF16),
        struct((group * (slots + rows), lines), BF16),
        struct((rows, slots), BF16),
        struct((lines, cache_size), F32),
    )
    pqt, pkt, pvt, spread, take, place, home, bias = call(
        functools.partial(prep_body, group),
        prepared,
        [SMEM, SMEM, HBM, HBM, HBM],
        (HBM,) * 8,
        scratch=[pltpu.VMEM(a.shape, a.dtype) for a in prepared]
        + [pltpu.VMEM(a.shape, a.dtype) for a in (plain_query_rows, plain_key_rows, plain_value_rows)]
        + [DMA((11,))],
        moved=6000000,
    )(dest, live_cache_length, plain_query_rows, plain_key_rows, plain_value_rows)

    down_here = lax.dynamic_slice_in_dim(stacked_down_weight[0], lax.axis_index("tp") * half, half, axis=1)
    rank_part = dot_t(received, down_here)
    terms = call(
        functools.partial(up_body, group),
        struct((slots, kv_heads * (group + 2) * head_dim), BF16),
        [VMEM] * 4,
        moved=2000000,
    )(rank_part, other_core(rank_part), query_up_weight, key_value_up_weight)
    returned = exchange(terms, wide_count)
    outgoing, context = call(
        functools.partial(attend_body, group),
        (struct((slots, query_width), BF16), struct((rows, query_width), BF16)),
        [VMEM] + [HBM] * 9,
        scratch=[pltpu.VMEM(a.shape, a.dtype) for a in (pqt, pkt, pvt, spread, take, place, bias)]
        + [pltpu.VMEM((kv_heads, rows, cache_size, head_dim), BF16)] * 2
        + [DMA((7 + 2 * kv_heads,))],
        moved=8000000,
        limit=58,
    )(returned, cached_key_rows, cached_value_rows, pqt, pkt, pvt, spread, take, place, bias)
    arrived = exchange(outgoing, wide_count)
    rank_o = dot_t(arrived, output_down_weight[0])
    out_terms = call(
        output_up_body, struct((slots, query_width), BF16), [VMEM] * 3, moved=1200000
    )(rank_o, other_core(rank_o), output_up_weight)
    adapter_output_term = call(
        unpack_body, struct((rows, query_width), BF16), [VMEM] * 2, moved=1000000
    )(home, exchange(out_terms, wide_count))
    return context, adapter_output_term


def solution(mesh):
    return jax.shard_map(
        shards,
        mesh=mesh,
        in_specs=(
            P(("groups", "wide"), None),
            P(("groups", "wide"), "tp"),
            P(("groups", "wide"), "tp"),
            P(("groups", "wide"), "tp"),
            P(("groups", "wide"), "tp", None, None),
            P(("groups", "wide"), "tp", None, None),
            P(("groups", "wide")),
            P("groups"),
            P("groups"),
            P("wide", None, None),
            P("wide", None, "tp"),
            P("wide", None, None, "tp"),
            P("wide", None, "tp"),
            P("wide", None, "tp"),
        ),
        out_specs=(P(("groups", "wide"), "tp"), P(("groups", "wide"), "tp")),
        check_vma=False,
    )
```

```python
import functools

import jax
import jax.numpy as jnp
from jax import lax
from jax.experimental import pallas as pl
from jax.experimental.pallas import tpu as pltpu
from jax.sharding import PartitionSpec as P

ADAPTER_SCALE = 0.5
F32 = jnp.float32
BF16 = jnp.bfloat16
VMEM = pl.BlockSpec(memory_space=pltpu.VMEM)
SMEM = pl.BlockSpec(memory_space=pltpu.SMEM)
HBM = pl.BlockSpec(memory_space=pltpu.HBM)
DMA = pltpu.SemaphoreType.DMA


def call(body, out_shape, in_specs, out_specs=None, scratch=(), flops=0, moved=0, limit=58):
    return pl.pallas_call(
        body,
        out_shape=out_shape,
        in_specs=in_specs,
        out_specs=jax.tree.map(lambda _: VMEM, out_shape) if out_specs is None else out_specs,
        scratch_shapes=scratch,
        cost_estimate=pl.CostEstimate(flops=flops, bytes_accessed=moved, transcendentals=0),
        compiler_params=pltpu.CompilerParams(vmem_limit_bytes=limit * 1024 * 1024),
    )


def iota(shape, dim):
    return lax.broadcasted_iota(jnp.int32, shape, dim)


def dot(a, b):
    return lax.dot_general(a, b, (((1,), (0,)), ((), ())), preferred_element_type=F32)


def dot_t(a, b):
    return lax.dot_general(a, b, (((1,), (1,)), ((), ())), preferred_element_type=F32)


def scalars_to_row(read, rows):
    lane = iota((1, rows), 1)
    row = jnp.zeros((1, rows), jnp.int32)
    for r in range(rows):
        row = jnp.where(lane == r, read(r), row)
    return row


def pack_body(
    capacity, tenant_hbm, slot_hbm, x_hbm, dest_ref, packed_ref, tenant_ref, slot_ref, count_ref, x_ref, sems
):
    slots, width = packed_ref.shape
    rows = x_ref.shape[0]
    start = pl.multiple_of(lax.axis_index("tp") * width, width)
    copies = [
        pltpu.make_async_copy(tenant_hbm, tenant_ref, sems.at[0]),
        pltpu.make_async_copy(slot_hbm, slot_ref, sems.at[1]),
        pltpu.make_async_copy(x_hbm.at[:, pl.ds(start, width)], x_ref, sems.at[2]),
    ]
    for copy in copies:
        copy.start()
    for d in range(slots // capacity):
        count_ref[d] = 0
    copies[0].wait()
    copies[1].wait()
    first = lax.axis_index("wide") * rows
    lane = iota((1, rows), 1)
    dest = jnp.zeros((1, rows), jnp.int32)
    for r in range(rows):
        holder = slot_ref[tenant_ref[first + r]]
        place = count_ref[holder]
        count_ref[holder] = place + 1
        slot = holder * capacity + place
        dest_ref[r] = slot
        dest = jnp.where(lane == r, slot, dest)
    chosen = (iota((slots, rows), 0) == dest).astype(F32).astype(BF16)
    copies[2].wait()
    packed_ref[...] = dot(chosen, x_ref[...]).astype(BF16)


def down_body(ret_ref, down_ref, out_ref):
    width = ret_ref.shape[1]
    start = pl.multiple_of(lax.axis_index("tp") * width, width)
    out_ref[...] = dot_t(ret_ref[...], down_ref[0, :, pl.ds(start, width)])


def up_body(group, mine_ref, other_ref, uq_ref, ukv_ref, out_ref):
    rank = uq_ref.shape[1]
    total = (mine_ref[...] + other_ref[...]).astype(BF16)
    q_width = uq_ref.shape[2]
    width = ukv_ref.shape[3]
    out_ref[:, :q_width] = dot(total[:, :rank], uq_ref[0]).astype(BF16)
    for i in range(2):
        out_ref[:, q_width + i * width : q_width + (i + 1) * width] = dot(
            total[:, (i + 1) * rank : (i + 2) * rank], ukv_ref[0, i]
        ).astype(BF16)


def attend_body(
    group, ret_ref, dest_ref, len_ref, pq_ref, pk_ref, pv_ref, k_ref, v_ref, packed_ref, context_hbm,
    context_ref, out_sems,
):
    rows, heads, cache_size, head_dim = k_ref.shape
    slots = packed_ref.shape[0]
    lines = rows * group
    shift = group.bit_length() - 1
    lane = iota((1, rows), 1)
    dest_row = jnp.zeros((1, rows), jnp.int32)
    len_row = jnp.zeros((1, rows), jnp.int32)
    for r in range(rows):
        dest_row = jnp.where(lane == r, dest_ref[r], dest_row)
        len_row = jnp.where(lane == r, len_ref[r], len_row)
    mine = (iota((lines, rows), 0) >> shift) == iota((lines, rows), 1)
    dest_line = jnp.sum(jnp.where(mine, dest_row, 0), axis=1, keepdims=True)
    len_line = jnp.sum(jnp.where(mine, len_row, 0), axis=1, keepdims=True)
    head_line = iota((lines, 1), 0) & (group - 1)
    row_line = iota((lines, 1), 0) >> shift
    to_line = (iota((lines, group * rows), 1) == head_line * rows + row_line).astype(F32).astype(BF16)
    repeat = mine.astype(F32).astype(BF16)
    spread = jnp.where(
        iota((lines, group * slots), 1) == head_line * slots + dest_line, ADAPTER_SCALE, 0.0
    ).astype(BF16)
    take = jnp.where(iota((lines, slots), 1) == dest_line, ADAPTER_SCALE, 0.0).astype(BF16)
    here = iota((rows, lines), 0) == (iota((rows, lines), 1) >> shift)
    eye = iota((rows, rows), 0) == iota((rows, rows), 1)
    dest_col = jnp.sum(jnp.where(eye, dest_row, 0), axis=1, keepdims=True)
    dest_lane = jnp.sum(jnp.where(here, dest_col, 0), axis=0, keepdims=True)
    head_lane = iota((1, lines), 1) & (group - 1)
    row_lane = iota((1, lines), 1) >> shift
    place_out = (iota((group * slots, lines), 0) == head_lane * slots + dest_lane).astype(F32).astype(BF16)
    place_home = (iota((group * rows, lines), 0) == head_lane * rows + row_lane).astype(F32).astype(BF16)
    bias = jnp.where(iota((lines, cache_size), 1) < len_line, 0.0, -jnp.inf)
    scale = head_dim ** (-0.5)
    k_base = heads * group * head_dim
    v_base = k_base + heads * head_dim
    lhs = jnp.concatenate([spread, to_line], axis=1)
    lhs_own = jnp.concatenate([take, repeat], axis=1)
    leaving = []
    for i in range(heads):
        g = i
        first = i * group * head_dim
        stacked = jnp.concatenate(
            [ret_ref[:, first + h * head_dim : first + (h + 1) * head_dim] for h in range(group)]
            + [pq_ref[:, first + h * head_dim : first + (h + 1) * head_dim] for h in range(group)],
            axis=0,
        )
        query = dot(lhs, stacked).astype(BF16).astype(F32)
        columns = slice(i * head_dim, (i + 1) * head_dim)
        new_key, new_value = (
            dot(lhs_own, jnp.concatenate([ret_ref[:, base + i * head_dim : base + (i + 1) * head_dim], plain[:, columns]], axis=0))
            .astype(BF16).astype(F32)
            for base, plain in ((k_base, pk_ref), (v_base, pv_ref))
        )
        own = jnp.sum(query * new_key, axis=1, keepdims=True) * scale
        score = jnp.concatenate(
            [dot_t(query[r * group : (r + 1) * group].astype(BF16), k_ref[r, g]) for r in range(rows)], axis=0
        )
        score = score * scale + bias
        highest = jnp.maximum(jnp.max(score, axis=1, keepdims=True), own)
        raised = jnp.exp(score - highest)
        own_raised = jnp.exp(own - highest)
        inverse = 1.0 / (jnp.sum(raised, axis=1, keepdims=True) + own_raised)
        weight = raised * inverse
        own_weight = (own_raised * inverse).astype(BF16).astype(F32)
        attended = jnp.concatenate(
            [dot(weight[r * group : (r + 1) * group].astype(BF16), v_ref[r, g]) for r in range(rows)], axis=0
        )
        context = (attended + own_weight * new_value).astype(BF16)
        laid_out = dot(place_out, context).astype(BF16)
        laid_home = dot(place_home, context).astype(BF16)
        for h in range(group):
            columns = slice((i * group + h) * head_dim, (i * group + h + 1) * head_dim)
            packed_ref[:, columns] = laid_out[h * slots : (h + 1) * slots]
            context_ref[:, columns] = laid_home[h * rows : (h + 1) * rows]
        columns = pl.ds(i * group * head_dim, group * head_dim)
        copy = pltpu.make_async_copy(context_ref.at[:, columns], context_hbm.at[:, columns], out_sems.at[i])
        copy.start()
        leaving.append(copy)
    for copy in leaving:
        copy.wait()


def output_up_body(mine_ref, other_ref, uo_ref, out_ref):
    total = (mine_ref[...] + other_ref[...]).astype(BF16)
    out_ref[...] = (ADAPTER_SCALE * dot(total, uo_ref[0])).astype(BF16)


def unpack_body(dest_ref, ret_ref, out_hbm, out_ref, sems):
    rows, width = out_ref.shape
    slots = ret_ref.shape[0]
    line = iota((rows, 1), 0)
    dest = jnp.zeros((rows, 1), jnp.int32)
    for r in range(rows):
        dest = jnp.where(line == r, dest_ref[r], dest)
    home = (iota((rows, slots), 1) == dest).astype(F32).astype(BF16)
    parts = sems.shape[0]
    part = width // parts
    leaving = []
    for i in range(parts):
        columns = pl.ds(i * part, part)
        out_ref[:, columns] = dot(home, ret_ref[:, columns]).astype(BF16)
        copy = pltpu.make_async_copy(out_ref.at[:, columns], out_hbm.at[:, columns], sems.at[i])
        copy.start()
        leaving.append(copy)
    for copy in leaving:
        copy.wait()


def exchange(rows, wide_count):
    slots, width = rows.shape
    moved = lax.all_to_all(
        rows.reshape(wide_count, slots // wide_count, width), "wide", split_axis=0, concat_axis=0, tiled=True
    )
    return moved.reshape(slots, width)


def other_core(value):
    return lax.ppermute(value, "tp", [(0, 1), (1, 0)])


def shards(
    normed_layer_input,
    plain_query_rows,
    plain_key_rows,
    plain_value_rows,
    cached_key_rows,
    cached_value_rows,
    live_cache_length,
    tenant,
    slot_of_adapter,
    stacked_down_weight,
    query_up_weight,
    key_value_up_weight,
    output_down_weight,
    output_up_weight,
):
    wide_count = lax.axis_size("wide")
    rows, features = normed_layer_input.shape
    half = features // lax.axis_size("tp")
    capacity = max(2, 2 * rows // wide_count)
    slots = wide_count * capacity
    kv_heads, cache_size, head_dim = cached_key_rows.shape[1:]
    query_width = plain_query_rows.shape[1]
    group = query_width // head_dim // kv_heads
    lines = rows * group
    struct = jax.ShapeDtypeStruct

    dest, packed = call(
        functools.partial(pack_body, capacity),
        (struct((rows,), jnp.int32), struct((slots, half), BF16)),
        [HBM, HBM, HBM],
        (SMEM, VMEM),
        scratch=[
            pltpu.SMEM(tenant.shape, jnp.int32),
            pltpu.SMEM(slot_of_adapter.shape, jnp.int32),
            pltpu.SMEM((wide_count,), jnp.int32),
            pltpu.VMEM((rows, half), BF16),
            DMA((3,)),
        ],
        moved=4 * slots * half,
    )(tenant, slot_of_adapter, normed_layer_input)
    received = exchange(packed, wide_count)

    rank_part = call(
        down_body, struct((slots, stacked_down_weight.shape[1]), F32), [VMEM] * 2, moved=4000000, limit=16
    )(received, stacked_down_weight)
    terms = call(
        functools.partial(up_body, group),
        struct((slots, kv_heads * (group + 2) * head_dim), BF16),
        [VMEM] * 4,
        moved=2000000,
        limit=16,
    )(rank_part, other_core(rank_part), query_up_weight, key_value_up_weight)
    returned = exchange(terms, wide_count)
    outgoing, context = call(
        functools.partial(attend_body, group),
        (struct((slots, query_width), BF16), struct((rows, query_width), BF16)),
        [VMEM, SMEM, SMEM, VMEM, VMEM, VMEM, VMEM, VMEM],
        (VMEM, HBM),
        scratch=[pltpu.VMEM((rows, query_width), BF16), DMA((kv_heads,))],
        moved=8000000,
        limit=16,
    )(
        returned, dest, live_cache_length, plain_query_rows, plain_key_rows, plain_value_rows,
        cached_key_rows, cached_value_rows,
    )
    arrived = exchange(outgoing, wide_count)
    rank_o = dot_t(arrived, output_down_weight[0])
    out_terms = call(
        output_up_body, struct((slots, query_width), BF16), [VMEM] * 3, moved=1200000, limit=16
    )(rank_o, other_core(rank_o), output_up_weight)
    adapter_output_term = call(
        unpack_body, struct((rows, query_width), BF16), [SMEM, VMEM], HBM,
        scratch=[pltpu.VMEM((rows, query_width), BF16), DMA((4,))], moved=1000000, limit=16,
    )(dest, exchange(out_terms, wide_count))
    return context, adapter_output_term


def solution(mesh):
    return jax.shard_map(
        shards,
        mesh=mesh,
        in_specs=(
            P(("groups", "wide"), None),
            P(("groups", "wide"), "tp"),
            P(("groups", "wide"), "tp"),
            P(("groups", "wide"), "tp"),
            P(("groups", "wide"), "tp", None, None),
            P(("groups", "wide"), "tp", None, None),
            P(("groups", "wide")),
            P("groups"),
            P("groups"),
            P("wide", None, None),
            P("wide", None, "tp"),
            P("wide", None, None, "tp"),
            P("wide", None, "tp"),
            P("wide", None, "tp"),
        ),
        out_specs=(P(("groups", "wide"), "tp"), P(("groups", "wide"), "tp")),
        check_vma=False,
    )
```

```python
import functools

import jax
import jax.numpy as jnp
from jax import lax
from jax.experimental import pallas as pl
from jax.experimental.pallas import tpu as pltpu
from jax.sharding import PartitionSpec as P

ADAPTER_SCALE = 0.5
F32 = jnp.float32
BF16 = jnp.bfloat16
VMEM = pl.BlockSpec(memory_space=pltpu.VMEM)
SMEM = pl.BlockSpec(memory_space=pltpu.SMEM)
HBM = pl.BlockSpec(memory_space=pltpu.HBM)
DMA = pltpu.SemaphoreType.DMA


def call(body, out_shape, in_specs, out_specs=None, scratch=(), flops=0, moved=0, limit=58):
    return pl.pallas_call(
        body,
        out_shape=out_shape,
        in_specs=in_specs,
        out_specs=jax.tree.map(lambda _: VMEM, out_shape) if out_specs is None else out_specs,
        scratch_shapes=scratch,
        cost_estimate=pl.CostEstimate(flops=flops, bytes_accessed=moved, transcendentals=0),
        compiler_params=pltpu.CompilerParams(vmem_limit_bytes=limit * 1024 * 1024),
    )


def iota(shape, dim):
    return lax.broadcasted_iota(jnp.int32, shape, dim)


def dot(a, b):
    return lax.dot_general(a, b, (((1,), (0,)), ((), ())), preferred_element_type=F32)


def dot_t(a, b):
    return lax.dot_general(a, b, (((1,), (1,)), ((), ())), preferred_element_type=F32)


def scalars_to_row(read, rows):
    lane = iota((1, rows), 1)
    row = jnp.zeros((1, rows), jnp.int32)
    for r in range(rows):
        row = jnp.where(lane == r, read(r), row)
    return row


def pack_body(
    capacity, tenant_hbm, slot_hbm, len_hbm, x_hbm, table_ref, packed_ref,
    tenant_ref, slot_ref, len_ref, count_ref, x_ref, sems,
):
    slots, width = packed_ref.shape
    rows = x_ref.shape[0]
    start = pl.multiple_of(lax.axis_index("tp") * width, width)
    copies = [
        pltpu.make_async_copy(tenant_hbm, tenant_ref, sems.at[0]),
        pltpu.make_async_copy(slot_hbm, slot_ref, sems.at[1]),
        pltpu.make_async_copy(len_hbm, len_ref, sems.at[3]),
        pltpu.make_async_copy(x_hbm.at[:, pl.ds(start, width)], x_ref, sems.at[2]),
    ]
    for copy in copies:
        copy.start()
    for d in range(slots // capacity):
        count_ref[d] = 0
    for copy in copies[:3]:
        copy.wait()
    first = lax.axis_index("wide") * rows
    lane = iota((1, rows), 1)
    dest = jnp.zeros((1, rows), jnp.int32)
    for r in range(rows):
        holder = slot_ref[tenant_ref[first + r]]
        place = count_ref[holder]
        count_ref[holder] = place + 1
        slot = holder * capacity + place
        table_ref[r] = slot
        table_ref[rows + r] = len_ref[r]
        dest = jnp.where(lane == r, slot, dest)
    chosen = (iota((slots, rows), 0) == dest).astype(F32).astype(BF16)
    copies[3].wait()
    packed_ref[...] = dot(chosen, x_ref[...]).astype(BF16)


def up_body(group, mine_ref, other_ref, uq_ref, ukv_ref, out_ref):
    rank = uq_ref.shape[1]
    total = (mine_ref[...] + other_ref[...]).astype(BF16)
    q_width = uq_ref.shape[2]
    width = ukv_ref.shape[3]
    out_ref[:, :q_width] = dot(total[:, :rank], uq_ref[0]).astype(BF16)
    for i in range(2):
        out_ref[:, q_width + i * width : q_width + (i + 1) * width] = dot(
            total[:, (i + 1) * rank : (i + 2) * rank], ukv_ref[0, i]
        ).astype(BF16)


def prep_body(
    group, table_ref, spread_ref, take_ref, out_ref, back_ref, home_ref, bias_ref,
):
    lines = spread_ref.shape[0]
    rows, slots = home_ref.shape
    shift = group.bit_length() - 1
    lane = iota((1, rows), 1)
    dest_row = jnp.zeros((1, rows), jnp.int32)
    len_row = jnp.zeros((1, rows), jnp.int32)
    for r in range(rows):
        dest_row = jnp.where(lane == r, table_ref[r], dest_row)
        len_row = jnp.where(lane == r, table_ref[rows + r], len_row)
    mine = (iota((lines, rows), 0) >> shift) == iota((lines, rows), 1)
    dest_line = jnp.sum(jnp.where(mine, dest_row, 0), axis=1, keepdims=True)
    len_line = jnp.sum(jnp.where(mine, len_row, 0), axis=1, keepdims=True)
    head_line = iota((lines, 1), 0) & (group - 1)
    row_line = iota((lines, 1), 0) >> shift
    to_line = (iota((lines, group * rows), 1) == head_line * rows + row_line).astype(F32).astype(BF16)
    repeat = mine.astype(F32).astype(BF16)
    taken = jnp.where(
        iota((lines, group * slots), 1) == head_line * slots + dest_line, ADAPTER_SCALE, 0.0
    ).astype(BF16)
    spread_ref[...] = jnp.concatenate([taken, to_line], axis=1)
    taken = jnp.where(iota((lines, slots), 1) == dest_line, ADAPTER_SCALE, 0.0).astype(BF16)
    take_ref[...] = jnp.concatenate([taken, repeat], axis=1)
    here = iota((rows, lines), 0) == (iota((rows, lines), 1) >> shift)
    eye = iota((rows, rows), 0) == iota((rows, rows), 1)
    dest_col = jnp.sum(jnp.where(eye, dest_row, 0), axis=1, keepdims=True)
    dest_lane = jnp.sum(jnp.where(here, dest_col, 0), axis=0, keepdims=True)
    head_lane = iota((1, lines), 1) & (group - 1)
    row_lane = iota((1, lines), 1) >> shift
    out_ref[...] = (iota((group * slots, lines), 0) == head_lane * slots + dest_lane).astype(F32).astype(BF16)
    back_ref[...] = (iota((group * rows, lines), 0) == head_lane * rows + row_lane).astype(F32).astype(BF16)
    home_ref[...] = (iota((rows, slots), 1) == dest_col).astype(F32).astype(BF16)
    bias_ref[...] = jnp.where(iota(bias_ref.shape, 1) < len_line, 0.0, -jnp.inf)


def attend_body(
    group, ret_ref, k_ref, v_ref, pq_ref, pk_ref, pv_ref, spread_ref, take_ref, out_ref, back_ref, home_ref, bias_ref,
    packed_ref, context_hbm, context_ref, out_sems,
):
    rows, heads, cache_size, head_dim = k_ref.shape
    slots = packed_ref.shape[0]
    spread, take, place_out, place_home = spread_ref[...], take_ref[...], out_ref[...], back_ref[...]
    bias = bias_ref[...]
    scale = head_dim ** (-0.5)
    k_base = heads * group * head_dim
    v_base = k_base + heads * head_dim
    leaving = []
    for i in range(heads):
        g = i
        first = i * group * head_dim
        stacked = jnp.concatenate(
            [
                source[:, first + h * head_dim : first + (h + 1) * head_dim]
                for source in (ret_ref, pq_ref)
                for h in range(group)
            ],
            axis=0,
        )
        query = dot(spread, stacked).astype(BF16).astype(F32)
        columns = slice(i * head_dim, (i + 1) * head_dim)
        new_key, new_value = (
            dot(
                take,
                jnp.concatenate(
                    [ret_ref[:, base + i * head_dim : base + (i + 1) * head_dim], plain[:, columns]], axis=0
                ),
            ).astype(BF16).astype(F32)
            for base, plain in ((k_base, pk_ref), (v_base, pv_ref))
        )
        own = jnp.sum(query * new_key, axis=1, keepdims=True) * scale
        score = jnp.concatenate(
            [dot_t(query[r * group : (r + 1) * group].astype(BF16), k_ref[r, g]) for r in range(rows)], axis=0
        )
        score = score * scale + bias
        highest = jnp.maximum(jnp.max(score, axis=1, keepdims=True), own)
        raised = jnp.exp(score - highest)
        own_raised = jnp.exp(own - highest)
        inverse = 1.0 / (jnp.sum(raised, axis=1, keepdims=True) + own_raised)
        weight = raised * inverse
        own_weight = (own_raised * inverse).astype(BF16).astype(F32)
        attended = jnp.concatenate(
            [dot(weight[r * group : (r + 1) * group].astype(BF16), v_ref[r, g]) for r in range(rows)], axis=0
        )
        context = (attended + own_weight * new_value).astype(BF16)
        laid_out = dot(place_out, context).astype(BF16)
        laid_home = dot(place_home, context).astype(BF16)
        for h in range(group):
            columns = slice((i * group + h) * head_dim, (i * group + h + 1) * head_dim)
            packed_ref[:, columns] = laid_out[h * slots : (h + 1) * slots]
            context_ref[:, columns] = laid_home[h * rows : (h + 1) * rows]
        columns = pl.ds(i * group * head_dim, group * head_dim)
        copy = pltpu.make_async_copy(context_ref.at[:, columns], context_hbm.at[:, columns], out_sems.at[i])
        copy.start()
        leaving.append(copy)
    for copy in leaving:
        copy.wait()


def output_up_body(mine_ref, other_ref, uo_ref, out_ref):
    total = (mine_ref[...] + other_ref[...]).astype(BF16)
    out_ref[...] = (ADAPTER_SCALE * dot(total, uo_ref[0])).astype(BF16)


def unpack_body(home_ref, ret_ref, out_hbm, out_ref, sems):
    rows, width = out_ref.shape
    home = home_ref[...]
    parts = sems.shape[0]
    part = width // parts
    leaving = []
    for i in range(parts):
        columns = pl.ds(i * part, part)
        out_ref[:, columns] = dot(home, ret_ref[:, columns]).astype(BF16)
        copy = pltpu.make_async_copy(out_ref.at[:, columns], out_hbm.at[:, columns], sems.at[i])
        copy.start()
        leaving.append(copy)
    for copy in leaving:
        copy.wait()


def exchange(rows, wide_count):
    slots, width = rows.shape
    moved = lax.all_to_all(
        rows.reshape(wide_count, slots // wide_count, width), "wide", split_axis=0, concat_axis=0, tiled=True
    )
    return moved.reshape(slots, width)


def other_core(value):
    return lax.ppermute(value, "tp", [(0, 1), (1, 0)])


def shards(
    normed_layer_input,
    plain_query_rows,
    plain_key_rows,
    plain_value_rows,
    cached_key_rows,
    cached_value_rows,
    live_cache_length,
    tenant,
    slot_of_adapter,
    stacked_down_weight,
    query_up_weight,
    key_value_up_weight,
    output_down_weight,
    output_up_weight,
):
    wide_count = lax.axis_size("wide")
    rows, features = normed_layer_input.shape
    half = features // lax.axis_size("tp")
    capacity = max(2, 2 * rows // wide_count)
    slots = wide_count * capacity
    kv_heads, cache_size, head_dim = cached_key_rows.shape[1:]
    query_width = plain_query_rows.shape[1]
    group = query_width // head_dim // kv_heads
    lines = rows * group
    struct = jax.ShapeDtypeStruct

    table, packed = call(
        functools.partial(pack_body, capacity),
        (struct((2 * rows,), jnp.int32), struct((slots, half), BF16)),
        [HBM] * 4,
        (SMEM, VMEM),
        scratch=[
            pltpu.SMEM(tenant.shape, jnp.int32),
            pltpu.SMEM(slot_of_adapter.shape, jnp.int32),
            pltpu.SMEM((rows,), jnp.int32),
            pltpu.SMEM((wide_count,), jnp.int32),
            pltpu.VMEM((rows, half), BF16),
            DMA((4,)),
        ],
        moved=4 * slots * half,
    )(tenant, slot_of_adapter, live_cache_length, normed_layer_input)
    packed, feature_start = lax.optimization_barrier((packed, lax.axis_index("tp").astype(jnp.uint32) * jnp.uint32(half)))
    received = exchange(packed, wide_count)

    down_here = lax.dynamic_slice(stacked_down_weight[0], (jnp.uint32(0), feature_start), (stacked_down_weight.shape[1], half))
    rank_part = dot_t(received, down_here)
    rank_other = other_core(rank_part)
    table, rank_part = lax.optimization_barrier((table, rank_part))
    prepared = (
        struct((lines, group * (slots + rows)), BF16),
        struct((lines, slots + rows), BF16),
        struct((group * slots, lines), BF16),
        struct((group * rows, lines), BF16),
        struct((rows, slots), BF16),
        struct((lines, cache_size), F32),
    )
    prepared = call(
        functools.partial(prep_body, group), prepared, [SMEM], moved=2000000, limit=16
    )(table)
    rank_other, prepared = lax.optimization_barrier((rank_other, prepared))
    home = prepared[4]
    terms = call(
        functools.partial(up_body, group),
        struct((slots, kv_heads * (group + 2) * head_dim), BF16),
        [VMEM] * 4,
        moved=20000000,
        flops=10**9,
        limit=16,
    )(rank_part, rank_other, query_up_weight, key_value_up_weight)
    returned = exchange(terms, wide_count)
    outgoing, context = call(
        functools.partial(attend_body, group),
        (struct((slots, query_width), BF16), struct((rows, query_width), BF16)),
        [VMEM] * (6 + len(prepared)),
        (VMEM, HBM),
        scratch=[pltpu.VMEM((rows, query_width), BF16), DMA((kv_heads,))],
        moved=8000000,
        limit=16,
    )(
        returned, cached_key_rows, cached_value_rows, plain_query_rows, plain_key_rows, plain_value_rows, *prepared
    )
    arrived = exchange(outgoing, wide_count)
    rank_o = dot_t(arrived, output_down_weight[0])
    out_terms = call(
        output_up_body, struct((slots, query_width), BF16), [VMEM] * 3, moved=1200000, limit=16
    )(rank_o, other_core(rank_o), output_up_weight)
    adapter_output_term = call(
        unpack_body, struct((rows, query_width), BF16), [VMEM, VMEM], HBM,
        scratch=[pltpu.VMEM((rows, query_width), BF16), DMA((4,))], moved=1000000, limit=16,
    )(home, exchange(out_terms, wide_count))
    return context, adapter_output_term


def solution(mesh):
    return jax.shard_map(
        shards,
        mesh=mesh,
        in_specs=(
            P(("groups", "wide"), None),
            P(("groups", "wide"), "tp"),
            P(("groups", "wide"), "tp"),
            P(("groups", "wide"), "tp"),
            P(("groups", "wide"), "tp", None, None),
            P(("groups", "wide"), "tp", None, None),
            P(("groups", "wide")),
            P("groups"),
            P("groups"),
            P("wide", None, None),
            P("wide", None, "tp"),
            P("wide", None, None, "tp"),
            P("wide", None, "tp"),
            P("wide", None, "tp"),
        ),
        out_specs=(P(("groups", "wide"), "tp"), P(("groups", "wide"), "tp")),
        check_vma=False,
    )
```

```python
import functools

import jax
import jax.numpy as jnp
from jax import lax
from jax.experimental import pallas as pl
from jax.experimental.pallas import tpu as pltpu
from jax.sharding import PartitionSpec as P

ADAPTER_SCALE = 0.5
F32 = jnp.float32
BF16 = jnp.bfloat16
VMEM = pl.BlockSpec(memory_space=pltpu.VMEM)
SMEM = pl.BlockSpec(memory_space=pltpu.SMEM)
HBM = pl.BlockSpec(memory_space=pltpu.HBM)
DMA = pltpu.SemaphoreType.DMA


def call(body, out_shape, in_specs, out_specs=None, scratch=(), flops=0, moved=0, limit=58):
    return pl.pallas_call(
        body,
        out_shape=out_shape,
        in_specs=in_specs,
        out_specs=jax.tree.map(lambda _: VMEM, out_shape) if out_specs is None else out_specs,
        scratch_shapes=scratch,
        cost_estimate=pl.CostEstimate(flops=flops, bytes_accessed=moved, transcendentals=0),
        compiler_params=pltpu.CompilerParams(vmem_limit_bytes=limit * 1024 * 1024),
    )


def iota(shape, dim):
    return lax.broadcasted_iota(jnp.int32, shape, dim)


def dot(a, b):
    return lax.dot_general(a, b, (((1,), (0,)), ((), ())), preferred_element_type=F32)


def dot_t(a, b):
    return lax.dot_general(a, b, (((1,), (1,)), ((), ())), preferred_element_type=F32)


def scalars(read, rows):
    lane = iota((1, rows), 1)
    row = jnp.zeros((1, rows), jnp.int32)
    for r in range(rows):
        row = jnp.where(lane == r, read(r), row)
    return row


def joined(refs):
    if len(refs) == 1:
        return refs[0][...]
    return jnp.concatenate([ref[...].astype(F32) for ref in reversed(refs)], axis=0).astype(BF16)


def store_blocks(refs, value, columns=slice(None)):
    rows = value.shape[0] // len(refs)
    for i, ref in enumerate(refs):
        first = (len(refs) - 1 - i) * rows
        ref[:, columns] = value[first : first + rows].astype(BF16)


def pack_body(capacity, by_distance, tenant_hbm, slot_hbm, len_hbm, x_hbm, table_ref, *refs):
    packed_refs, (tenant_ref, slot_ref, len_ref, count_ref, x_ref, sems) = refs[:-6], refs[-6:]
    slots = sum(ref.shape[0] for ref in packed_refs)
    rows, width = x_ref.shape
    here = lax.axis_index("wide") if by_distance else 0
    start = pl.multiple_of(lax.axis_index("tp") * width, width)
    copies = [
        pltpu.make_async_copy(tenant_hbm, tenant_ref, sems.at[0]),
        pltpu.make_async_copy(slot_hbm, slot_ref, sems.at[1]),
        pltpu.make_async_copy(len_hbm, len_ref, sems.at[3]),
        pltpu.make_async_copy(x_hbm.at[:, pl.ds(start, width)], x_ref, sems.at[2]),
    ]
    for copy in copies:
        copy.start()
    for d in range(slots // capacity):
        count_ref[d] = 0
    for copy in copies[:3]:
        copy.wait()
    first = lax.axis_index("wide") * rows
    lane = iota((1, rows), 1)
    dest = jnp.zeros((1, rows), jnp.int32)
    for r in range(rows):
        holder = slot_ref[tenant_ref[first + r]]
        place = count_ref[holder]
        count_ref[holder] = place + 1
        slot = (holder ^ here) * capacity + place
        table_ref[r] = slot
        table_ref[rows + r] = len_ref[r]
        dest = jnp.where(lane == r, slot, dest)
    chosen = (iota((slots, rows), 0) == dest).astype(F32).astype(BF16)
    copies[3].wait()
    store_blocks(packed_refs, dot(chosen, x_ref[...]))


def down_body(ret_refs, down_ref, out_ref):
    rows = joined(ret_refs)
    width = rows.shape[1]
    start = pl.multiple_of(lax.axis_index("tp") * width, width)
    out_ref[...] = dot_t(rows, down_ref[0, :, pl.ds(start, width)])


def output_down_body(ret_refs, down_ref, out_ref):
    out_ref[...] = dot_t(joined(ret_refs), down_ref[0])


def up_body(group, mine_ref, other_ref, uq_ref, ukv_ref, *out_refs):
    rank = uq_ref.shape[1]
    total = (mine_ref[...] + other_ref[...]).astype(BF16)
    q_width = uq_ref.shape[2]
    width = ukv_ref.shape[3]
    store_blocks(out_refs, dot(total[:, :rank], uq_ref[0]), slice(0, q_width))
    for i in range(2):
        store_blocks(
            out_refs,
            dot(total[:, (i + 1) * rank : (i + 2) * rank], ukv_ref[0, i]),
            slice(q_width + i * width, q_width + (i + 1) * width),
        )


def prep_body(group, table_ref, bias_ref, take_ref, send_ref, home_ref):
    lines = bias_ref.shape[0]
    rows, slots = home_ref.shape
    shift = group.bit_length() - 1
    dest_row = scalars(lambda r: table_ref[r], rows)
    len_row = scalars(lambda r: table_ref[rows + r], rows)
    mine = (iota((lines, rows), 0) >> shift) == iota((lines, rows), 1)
    len_line = jnp.sum(jnp.where(mine, len_row, 0), axis=1, keepdims=True)
    eye = iota((rows, rows), 0) == iota((rows, rows), 1)
    dest_col = jnp.sum(jnp.where(eye, dest_row, 0), axis=1, keepdims=True)
    bias_ref[...] = jnp.where(iota(bias_ref.shape, 1) < len_line, 0.0, -jnp.inf)
    at_home = iota((rows, slots), 1) == dest_col
    take_ref[...] = jnp.where(at_home, ADAPTER_SCALE, 0.0).astype(BF16)
    send_ref[...] = (iota((slots, rows), 0) == dest_row).astype(F32).astype(BF16)
    home_ref[...] = at_home.astype(F32).astype(BF16)


def attend_body(
    group, ret_refs, k_ref, v_ref, pq_ref, pk_ref, pv_ref, bias_ref, take_ref, send_ref, home_ref, *refs,
):
    packed_refs, (context_ref, ret_ref, line_ref) = refs[:-3], refs[-3:]
    ret_ref[...] = joined(ret_refs)
    rows, heads, cache_size, head_dim = k_ref.shape
    take, send = take_ref[...], send_ref[...]
    bias = bias_ref[...]
    scale = head_dim ** (-0.5)
    k_base = heads * group * head_dim
    v_base = k_base + heads * head_dim

    def lines_of(slot, part):
        for h in range(group):
            line_ref[slot, pl.ds(h, rows, stride=group), :] = part(h)
        return line_ref[slot]

    for g in range(heads):
        slot = 4 * (g % 2)
        columns = slice(g * group * head_dim, (g + 1) * group * head_dim)
        query_rows = pq_ref[:, columns].astype(F32) + dot(take, ret_ref[:, columns])
        query = lines_of(slot, lambda h: query_rows[:, h * head_dim : (h + 1) * head_dim])
        query = query.astype(BF16).astype(F32)
        key_columns = slice(g * head_dim, (g + 1) * head_dim)
        new_key, new_value = (
            (
                plain[:, key_columns].astype(F32)
                + dot(take, ret_ref[:, base + g * head_dim : base + (g + 1) * head_dim])
            ).astype(BF16).astype(F32)
            for base, plain in ((k_base, pk_ref), (v_base, pv_ref))
        )
        new_key = lines_of(slot + 1, lambda h: new_key)
        new_value = lines_of(slot + 2, lambda h: new_value)
        own = jnp.sum(query * new_key, axis=1, keepdims=True) * scale
        score = jnp.concatenate(
            [dot_t(query[r * group : (r + 1) * group].astype(BF16), k_ref[r, g]) for r in range(rows)], axis=0
        )
        score = score * scale + bias
        highest = jnp.maximum(jnp.max(score, axis=1, keepdims=True), own)
        raised = jnp.exp(score - highest)
        own_raised = jnp.exp(own - highest)
        inverse = 1.0 / (jnp.sum(raised, axis=1, keepdims=True) + own_raised)
        weight = raised * inverse
        own_weight = (own_raised * inverse).astype(BF16).astype(F32)
        attended = jnp.concatenate(
            [dot(weight[r * group : (r + 1) * group].astype(BF16), v_ref[r, g]) for r in range(rows)], axis=0
        )
        line_ref[slot + 3] = attended + own_weight * new_value
        context = jnp.concatenate(
            [line_ref[slot + 3, pl.ds(h, rows, stride=group), :] for h in range(group)], axis=1
        ).astype(BF16)
        context_ref[:, columns] = context
        store_blocks(packed_refs, dot(send, context), columns)


def output_up_body(mine_ref, other_ref, uo_ref, *out_refs):
    total = (mine_ref[...] + other_ref[...]).astype(BF16)
    store_blocks(out_refs, ADAPTER_SCALE * dot(total, uo_ref[0]))


def unpack_body(home_ref, ret_refs, out_hbm, out_ref, sems):
    rows, width = out_ref.shape
    home = home_ref[...]
    returned = joined(ret_refs)
    parts = sems.shape[0]
    part = width // parts
    leaving = []
    for i in range(parts):
        columns = slice(i * part, (i + 1) * part)
        out_ref[:, columns] = dot(home, returned[:, columns]).astype(BF16)
        copy = pltpu.make_async_copy(out_ref.at[:, columns], out_hbm.at[:, columns], sems.at[i])
        copy.start()
        leaving.append(copy)
    for copy in leaving:
        copy.wait()


def exchange(blocks, wide_count):
    if len(blocks) == 1:
        slots, width = blocks[0].shape
        moved = lax.all_to_all(
            blocks[0].reshape(wide_count, slots // wide_count, width), "wide", split_axis=0, concat_axis=0, tiled=True
        )
        return (moved.reshape(slots, width),)
    moved = [
        lax.ppermute(block, "wide", [(k, k ^ (wide_count - 1 - i)) for k in range(wide_count)])
        for i, block in enumerate(blocks[:-1])
    ]
    return (*moved, blocks[-1])


def other_core(value):
    return lax.ppermute(value, "tp", [(0, 1), (1, 0)])


def shards(
    normed_layer_input,
    plain_query_rows,
    plain_key_rows,
    plain_value_rows,
    cached_key_rows,
    cached_value_rows,
    live_cache_length,
    tenant,
    slot_of_adapter,
    stacked_down_weight,
    query_up_weight,
    key_value_up_weight,
    output_down_weight,
    output_up_weight,
):
    wide_count = lax.axis_size("wide")
    rows, features = normed_layer_input.shape
    half = features // lax.axis_size("tp")
    capacity = max(2, 2 * rows // wide_count)
    slots = wide_count * capacity
    kv_heads, cache_size, head_dim = cached_key_rows.shape[1:]
    query_width = plain_query_rows.shape[1]
    group = query_width // head_dim // kv_heads
    lines = rows * group
    by_distance = wide_count <= 8 and wide_count & (wide_count - 1) == 0
    count = wide_count if by_distance else 1
    struct = jax.ShapeDtypeStruct

    def blocks_of(width):
        return [struct((slots // count, width), BF16)] * count


    table, *packed = call(
        functools.partial(pack_body, capacity, by_distance),
        (struct((2 * rows,), jnp.int32), *blocks_of(half)),
        [HBM] * 4,
        (SMEM, *[VMEM] * count),
        scratch=[
            pltpu.SMEM(tenant.shape, jnp.int32),
            pltpu.SMEM(slot_of_adapter.shape, jnp.int32),
            pltpu.SMEM((rows,), jnp.int32),
            pltpu.SMEM((wide_count,), jnp.int32),
            pltpu.VMEM((rows, half), BF16),
            DMA((4,)),
        ],
        flops=10**9,
        moved=40000000,
    )(tenant, slot_of_adapter, live_cache_length, normed_layer_input)
    received = exchange(packed, wide_count)
    rank_part = call(
        down_body, struct((slots, stacked_down_weight.shape[1]), F32), [(VMEM,) * count, VMEM], moved=4000000, limit=16
    )(received, stacked_down_weight)
    rank_other = other_core(rank_part)
    table, rank_part = lax.optimization_barrier((table, rank_part))
    prepared = (
        struct((lines, cache_size), F32),
        struct((rows, slots), BF16),
        struct((slots, rows), BF16),
        struct((rows, slots), BF16),
    )
    prepared = call(
        functools.partial(prep_body, group), prepared, [SMEM], flops=10**9, moved=20000000, limit=16
    )(table)
    rank_other, prepared = lax.optimization_barrier((rank_other, prepared))
    home = prepared[3]
    terms = call(
        functools.partial(up_body, group),
        blocks_of(kv_heads * (group + 2) * head_dim),
        [VMEM] * 4,
        moved=20000000,
        flops=10**9,
        limit=16,
    )(rank_part, rank_other, query_up_weight, key_value_up_weight)
    returned = exchange(terms, wide_count)
    *outgoing, context = call(
        functools.partial(attend_body, group),
        [*blocks_of(query_width), struct((rows, query_width), BF16)],
        [(VMEM,) * count] + [VMEM] * (5 + len(prepared)),
        scratch=[
            pltpu.VMEM((slots, kv_heads * (group + 2) * head_dim), BF16),
            pltpu.VMEM((8, lines, head_dim), F32),
        ],
        moved=8000000,
        limit=16,
    )(
        returned, cached_key_rows, cached_value_rows, plain_query_rows, plain_key_rows, plain_value_rows, *prepared
    )
    arrived = exchange(outgoing, wide_count)
    rank_o = call(
        output_down_body, struct((slots, output_down_weight.shape[1]), F32), [(VMEM,) * count, VMEM], moved=4000000, limit=16
    )(arrived, output_down_weight)
    out_terms = call(
        output_up_body, blocks_of(query_width), [VMEM] * 3, moved=1200000, limit=16
    )(rank_o, other_core(rank_o), output_up_weight)
    adapter_output_term = call(
        unpack_body, struct((rows, query_width), BF16), [VMEM, (VMEM,) * count], HBM,
        scratch=[pltpu.VMEM((rows, query_width), BF16), DMA((4,))], moved=1000000, limit=16,
    )(home, exchange(out_terms, wide_count))
    return context, adapter_output_term


def solution(mesh):
    return jax.shard_map(
        shards,
        mesh=mesh,
        in_specs=(
            P(("groups", "wide"), None),
            P(("groups", "wide"), "tp"),
            P(("groups", "wide"), "tp"),
            P(("groups", "wide"), "tp"),
            P(("groups", "wide"), "tp", None, None),
            P(("groups", "wide"), "tp", None, None),
            P(("groups", "wide")),
            P("groups"),
            P("groups"),
            P("wide", None, None),
            P("wide", None, "tp"),
            P("wide", None, None, "tp"),
            P("wide", None, "tp"),
            P("wide", None, "tp"),
        ),
        out_specs=(P(("groups", "wide"), "tp"), P(("groups", "wide"), "tp")),
        check_vma=False,
    )
```

```python
import functools

import jax
import jax.numpy as jnp
from jax import lax
from jax.experimental import pallas as pl
from jax.experimental.pallas import tpu as pltpu
from jax.sharding import PartitionSpec as P

ADAPTER_SCALE = 0.5
F32 = jnp.float32
BF16 = jnp.bfloat16
VMEM = pl.BlockSpec(memory_space=pltpu.VMEM)
SMEM = pl.BlockSpec(memory_space=pltpu.SMEM)
HBM = pl.BlockSpec(memory_space=pltpu.HBM)
DMA = pltpu.SemaphoreType.DMA


def call(body, out_shape, in_specs, out_specs=None, scratch=(), flops=0, moved=0, limit=58):
    return pl.pallas_call(
        body,
        out_shape=out_shape,
        in_specs=in_specs,
        out_specs=jax.tree.map(lambda _: VMEM, out_shape) if out_specs is None else out_specs,
        scratch_shapes=scratch,
        cost_estimate=pl.CostEstimate(flops=flops, bytes_accessed=moved, transcendentals=0),
        compiler_params=pltpu.CompilerParams(vmem_limit_bytes=limit * 1024 * 1024),
    )


def iota(shape, dim):
    return lax.broadcasted_iota(jnp.int32, shape, dim)


def dot(a, b):
    return lax.dot_general(a, b, (((1,), (0,)), ((), ())), preferred_element_type=F32)


def dot_t(a, b):
    return lax.dot_general(a, b, (((1,), (1,)), ((), ())), preferred_element_type=F32)


def scalars(read, rows):
    lane = iota((1, rows), 1)
    row = jnp.zeros((1, rows), jnp.int32)
    for r in range(rows):
        row = jnp.where(lane == r, read(r), row)
    return row


def distances(count):
    return sorted(range(1, count), key=lambda d: (d >> 1 & 1, d), reverse=True) + [0]


def joined(refs):
    if len(refs) == 1:
        return refs[0][...]
    listed = sorted(zip(distances(len(refs)), refs), key=lambda pair: pair[0])
    return jnp.concatenate([ref[...].astype(F32) for _, ref in listed], axis=0).astype(BF16)


def store_blocks(refs, value, columns=slice(None)):
    rows = value.shape[0] // len(refs)
    for d, ref in zip(distances(len(refs)), refs):
        ref[:, columns] = value[d * rows : (d + 1) * rows].astype(BF16)


def pack_body(capacity, by_distance, tenant_hbm, slot_hbm, len_hbm, x_hbm, table_ref, *refs):
    packed_refs, (tenant_ref, slot_ref, len_ref, x_ref, sems) = refs[:-5], refs[-5:]
    slots = sum(ref.shape[0] for ref in packed_refs)
    rows, width = x_ref.shape
    here = lax.axis_index("wide") if by_distance else 0
    start = pl.multiple_of(lax.axis_index("tp") * width, width)
    copies = [
        pltpu.make_async_copy(tenant_hbm, tenant_ref, sems.at[0]),
        pltpu.make_async_copy(slot_hbm, slot_ref, sems.at[1]),
        pltpu.make_async_copy(len_hbm, len_ref, sems.at[3]),
        pltpu.make_async_copy(x_hbm.at[:, pl.ds(start, width)], x_ref, sems.at[2]),
    ]
    for copy in copies:
        copy.start()
    for copy in copies[:3]:
        copy.wait()
    first = lax.axis_index("wide") * rows
    holder = scalars(lambda r: slot_ref[tenant_ref[first + r]], rows)
    sublane, lane = iota((rows, rows), 0), iota((rows, rows), 1)
    holder_col = jnp.sum(jnp.where(sublane == lane, holder, 0), axis=1, keepdims=True)
    earlier = (holder_col == holder) & (sublane < lane)
    place = jnp.sum(earlier.astype(jnp.int32), axis=0, keepdims=True)
    dest = (holder ^ here) * capacity + place
    table_ref[0:1] = dest
    table_ref[1:2] = scalars(lambda r: len_ref[r], rows)
    chosen = (iota((slots, rows), 0) == dest).astype(F32).astype(BF16)
    copies[3].wait()
    store_blocks(packed_refs, dot(chosen, x_ref[...]))


def down_body(ret_refs, down_ref, out_ref):
    rows = joined(ret_refs)
    width = rows.shape[1]
    start = pl.multiple_of(lax.axis_index("tp") * width, width)
    out_ref[...] = dot_t(rows, down_ref[0, :, pl.ds(start, width)])


def output_down_body(ret_refs, down_ref, out_ref):
    out_ref[...] = dot_t(joined(ret_refs), down_ref[0])


def up_body(group, mine_ref, other_ref, uq_ref, ukv_ref, *out_refs):
    rank = uq_ref.shape[1]
    total = (mine_ref[...] + other_ref[...]).astype(BF16)
    q_width = uq_ref.shape[2]
    width = ukv_ref.shape[3]
    store_blocks(out_refs, dot(total[:, :rank], uq_ref[0]), slice(0, q_width))
    for i in range(2):
        store_blocks(
            out_refs,
            dot(total[:, (i + 1) * rank : (i + 2) * rank], ukv_ref[0, i]),
            slice(q_width + i * width, q_width + (i + 1) * width),
        )


def prep_body(group, table_ref, bias_ref, take_ref, send_ref, home_ref):
    lines = bias_ref.shape[0]
    rows, slots = home_ref.shape
    shift = group.bit_length() - 1
    dest_row, len_row = table_ref[0:1], table_ref[1:2]
    mine = (iota((lines, rows), 0) >> shift) == iota((lines, rows), 1)
    len_line = jnp.sum(jnp.where(mine, len_row, 0), axis=1, keepdims=True)
    eye = iota((rows, rows), 0) == iota((rows, rows), 1)
    dest_col = jnp.sum(jnp.where(eye, dest_row, 0), axis=1, keepdims=True)
    bias_ref[...] = jnp.where(iota(bias_ref.shape, 1) < len_line, 0.0, -jnp.inf)
    at_home = iota((rows, slots), 1) == dest_col
    take_ref[...] = jnp.where(at_home, ADAPTER_SCALE, 0.0).astype(BF16)
    send_ref[...] = (iota((slots, rows), 0) == dest_row).astype(F32).astype(BF16)
    home_ref[...] = at_home.astype(F32).astype(BF16)


def attend_body(
    group, ret_refs, k_ref, v_ref, pq_ref, pk_ref, pv_ref, bias_ref, take_ref, send_ref, home_ref, *refs,
):
    packed_refs, (context_ref, ret_ref, line_ref) = refs[:-3], refs[-3:]
    ret_ref[...] = joined(ret_refs)
    rows, heads, cache_size, head_dim = k_ref.shape
    take, send = take_ref[...], send_ref[...]
    bias = bias_ref[...]
    scale = head_dim ** (-0.5)
    k_base = heads * group * head_dim
    v_base = k_base + heads * head_dim

    def lines_of(slot, part):
        for h in range(group):
            line_ref[slot, pl.ds(h, rows, stride=group), :] = part(h)
        return line_ref[slot]

    def beside(value, r, side):
        lines = value[r * group : (r + 1) * group]
        pair = [jnp.zeros_like(lines)] * 2
        pair[side] = lines
        return jnp.concatenate(pair, axis=1)

    for g in range(heads):
        slot = 4 * (g % 2)
        columns = slice(g * group * head_dim, (g + 1) * group * head_dim)
        query_rows = pq_ref[:, columns].astype(F32) + dot(take, ret_ref[:, columns])
        query = lines_of(slot, lambda h: query_rows[:, h * head_dim : (h + 1) * head_dim])
        query = query.astype(BF16).astype(F32)
        key_columns = slice(g * head_dim, (g + 1) * head_dim)
        new_key, new_value = (
            (
                plain[:, key_columns].astype(F32)
                + dot(take, ret_ref[:, base + g * head_dim : base + (g + 1) * head_dim])
            ).astype(BF16).astype(F32)
            for base, plain in ((k_base, pk_ref), (v_base, pv_ref))
        )
        new_key = lines_of(slot + 1, lambda h: new_key)
        new_value = lines_of(slot + 2, lambda h: new_value)
        own = jnp.sum(query * new_key, axis=1, keepdims=True) * scale
        score = jnp.concatenate(
            [
                dot_t(
                    jnp.concatenate([beside(query, r, 0), beside(query, r + 1, 1)], axis=0).astype(BF16),
                    jnp.concatenate([k_ref[r, g], k_ref[r + 1, g]], axis=1),
                )
                for r in range(0, rows, 2)
            ],
            axis=0,
        )
        score = score * scale + bias
        highest = jnp.maximum(jnp.max(score, axis=1, keepdims=True), own)
        raised = jnp.exp(score - highest)
        own_raised = jnp.exp(own - highest)
        inverse = 1.0 / (jnp.sum(raised, axis=1, keepdims=True) + own_raised)
        weight = raised * inverse
        own_weight = (own_raised * inverse).astype(BF16).astype(F32)
        attended = jnp.concatenate(
            [dot(weight[r * group : (r + 1) * group].astype(BF16), v_ref[r, g]) for r in range(rows)], axis=0
        )
        line_ref[slot + 3] = attended + own_weight * new_value
        context = jnp.concatenate(
            [line_ref[slot + 3, pl.ds(h, rows, stride=group), :] for h in range(group)], axis=1
        ).astype(BF16)
        context_ref[:, columns] = context
        store_blocks(packed_refs, dot(send, context), columns)


def output_up_body(mine_ref, other_ref, uo_ref, *out_refs):
    total = (mine_ref[...] + other_ref[...]).astype(BF16)
    store_blocks(out_refs, ADAPTER_SCALE * dot(total, uo_ref[0]))


def unpack_body(home_ref, ret_refs, out_hbm, out_ref, sems):
    rows, width = out_ref.shape
    home = home_ref[...]
    returned = joined(ret_refs)
    parts = sems.shape[0]
    part = width // parts
    leaving = []
    for i in range(parts):
        columns = slice(i * part, (i + 1) * part)
        out_ref[:, columns] = dot(home, returned[:, columns]).astype(BF16)
        copy = pltpu.make_async_copy(out_ref.at[:, columns], out_hbm.at[:, columns], sems.at[i])
        copy.start()
        leaving.append(copy)
    for copy in leaving:
        copy.wait()


def exchange(blocks, wide_count):
    if len(blocks) == 1:
        slots, width = blocks[0].shape
        moved = lax.all_to_all(
            blocks[0].reshape(wide_count, slots // wide_count, width), "wide", split_axis=0, concat_axis=0, tiled=True
        )
        return (moved.reshape(slots, width),)
    moved = [
        lax.ppermute(block, "wide", [(k, k ^ d) for k in range(wide_count)])
        for d, block in zip(distances(wide_count), blocks[:-1])
    ]
    return (*moved, blocks[-1])


def other_core(value):
    return lax.ppermute(value, "tp", [(0, 1), (1, 0)])


def shards(
    normed_layer_input,
    plain_query_rows,
    plain_key_rows,
    plain_value_rows,
    cached_key_rows,
    cached_value_rows,
    live_cache_length,
    tenant,
    slot_of_adapter,
    stacked_down_weight,
    query_up_weight,
    key_value_up_weight,
    output_down_weight,
    output_up_weight,
):
    wide_count = lax.axis_size("wide")
    rows, features = normed_layer_input.shape
    half = features // lax.axis_size("tp")
    capacity = max(2, 2 * rows // wide_count)
    slots = wide_count * capacity
    kv_heads, cache_size, head_dim = cached_key_rows.shape[1:]
    query_width = plain_query_rows.shape[1]
    group = query_width // head_dim // kv_heads
    lines = rows * group
    by_distance = wide_count <= 8 and wide_count & (wide_count - 1) == 0
    count = wide_count if by_distance else 1
    struct = jax.ShapeDtypeStruct

    def blocks_of(width):
        return [struct((slots // count, width), BF16)] * count


    table, *packed = call(
        functools.partial(pack_body, capacity, by_distance),
        (struct((2, rows), jnp.int32), *blocks_of(half)),
        [HBM] * 4,
        scratch=[
            pltpu.SMEM(tenant.shape, jnp.int32),
            pltpu.SMEM(slot_of_adapter.shape, jnp.int32),
            pltpu.SMEM((rows,), jnp.int32),
            pltpu.VMEM((rows, half), BF16),
            DMA((4,)),
        ],
        flops=10**9,
        moved=40000000,
    )(tenant, slot_of_adapter, live_cache_length, normed_layer_input)
    received = exchange(packed, wide_count)
    prepared = (
        struct((lines, cache_size), F32),
        struct((rows, slots), BF16),
        struct((slots, rows), BF16),
        struct((rows, slots), BF16),
    )
    prepared = call(
        functools.partial(prep_body, group), prepared, [VMEM], flops=10**9, moved=20000000, limit=16
    )(table)
    received, prepared = lax.optimization_barrier((received, prepared))
    rank_part = call(
        down_body, struct((slots, stacked_down_weight.shape[1]), F32), [(VMEM,) * count, VMEM], moved=4000000, limit=16
    )(received, stacked_down_weight)
    rank_other = other_core(rank_part)
    home = prepared[3]
    terms = call(
        functools.partial(up_body, group),
        blocks_of(kv_heads * (group + 2) * head_dim),
        [VMEM] * 4,
        moved=20000000,
        flops=10**9,
        limit=16,
    )(rank_part, rank_other, query_up_weight, key_value_up_weight)
    returned = exchange(terms, wide_count)
    *outgoing, context = call(
        functools.partial(attend_body, group),
        [*blocks_of(query_width), struct((rows, query_width), BF16)],
        [(VMEM,) * count] + [VMEM] * (5 + len(prepared)),
        scratch=[
            pltpu.VMEM((slots, kv_heads * (group + 2) * head_dim), BF16),
            pltpu.VMEM((8, lines, head_dim), F32),
        ],
        moved=8000000,
        limit=16,
    )(
        returned, cached_key_rows, cached_value_rows, plain_query_rows, plain_key_rows, plain_value_rows, *prepared
    )
    arrived = exchange(outgoing, wide_count)
    rank_o = call(
        output_down_body, struct((slots, output_down_weight.shape[1]), F32), [(VMEM,) * count, VMEM], moved=4000000, limit=16
    )(arrived, output_down_weight)
    out_terms = call(
        output_up_body, blocks_of(query_width), [VMEM] * 3, moved=1200000, limit=16
    )(rank_o, other_core(rank_o), output_up_weight)
    adapter_output_term = call(
        unpack_body, struct((rows, query_width), BF16), [VMEM, (VMEM,) * count], HBM,
        scratch=[pltpu.VMEM((rows, query_width), BF16), DMA((4,))], moved=1000000, limit=16,
    )(home, exchange(out_terms, wide_count))
    return context, adapter_output_term


def solution(mesh):
    return jax.shard_map(
        shards,
        mesh=mesh,
        in_specs=(
            P(("groups", "wide"), None),
            P(("groups", "wide"), "tp"),
            P(("groups", "wide"), "tp"),
            P(("groups", "wide"), "tp"),
            P(("groups", "wide"), "tp", None, None),
            P(("groups", "wide"), "tp", None, None),
            P(("groups", "wide")),
            P("groups"),
            P("groups"),
            P("wide", None, None),
            P("wide", None, "tp"),
            P("wide", None, None, "tp"),
            P("wide", None, "tp"),
            P("wide", None, "tp"),
        ),
        out_specs=(P(("groups", "wide"), "tp"), P(("groups", "wide"), "tp")),
        check_vma=False,
    )
```

```python
import functools

import jax
import jax.numpy as jnp
from jax import lax
from jax.experimental import pallas as pl
from jax.experimental.pallas import tpu as pltpu
from jax.sharding import PartitionSpec as P

ADAPTER_SCALE = 0.5
F32 = jnp.float32
BF16 = jnp.bfloat16
VMEM = pl.BlockSpec(memory_space=pltpu.VMEM)
SMEM = pl.BlockSpec(memory_space=pltpu.SMEM)
HBM = pl.BlockSpec(memory_space=pltpu.HBM)
DMA = pltpu.SemaphoreType.DMA


def call(body, out_shape, in_specs, out_specs=None, scratch=(), flops=0, moved=0, limit=58):
    return pl.pallas_call(
        body,
        out_shape=out_shape,
        in_specs=in_specs,
        out_specs=jax.tree.map(lambda _: VMEM, out_shape) if out_specs is None else out_specs,
        scratch_shapes=scratch,
        cost_estimate=pl.CostEstimate(flops=flops, bytes_accessed=moved, transcendentals=0),
        compiler_params=pltpu.CompilerParams(vmem_limit_bytes=limit * 1024 * 1024),
    )


def iota(shape, dim):
    return lax.broadcasted_iota(jnp.int32, shape, dim)


def dot(a, b):
    return lax.dot_general(a, b, (((1,), (0,)), ((), ())), preferred_element_type=F32)


def dot_t(a, b):
    return lax.dot_general(a, b, (((1,), (1,)), ((), ())), preferred_element_type=F32)


def scalars(read, rows):
    lane = iota((1, rows), 1)
    row = jnp.zeros((1, rows), jnp.int32)
    for r in range(rows):
        row = jnp.where(lane == r, read(r), row)
    return row


def distances(count):
    return sorted(range(1, count), key=lambda d: (d >> 1 & 1, d), reverse=True) + [0]


def joined(refs):
    if len(refs) == 1:
        return refs[0][...]
    listed = sorted(zip(distances(len(refs)), refs), key=lambda pair: pair[0])
    return jnp.concatenate([ref[...].astype(F32) for _, ref in listed], axis=0).astype(BF16)


def store_blocks(refs, value, columns=slice(None)):
    rows = value.shape[0] // len(refs)
    for d, ref in zip(distances(len(refs)), refs):
        ref[:, columns] = value[d * rows : (d + 1) * rows].astype(BF16)


def pack_body(capacity, by_distance, tenant_hbm, slot_hbm, len_hbm, x_hbm, table_ref, *refs):
    packed_refs, (tenant_ref, slot_ref, len_ref, x_ref, sems) = refs[:-5], refs[-5:]
    slots = sum(ref.shape[0] for ref in packed_refs)
    rows, width = x_ref.shape
    here = lax.axis_index("wide") if by_distance else 0
    start = pl.multiple_of(lax.axis_index("tp") * width, width)
    copies = [
        pltpu.make_async_copy(tenant_hbm, tenant_ref, sems.at[0]),
        pltpu.make_async_copy(slot_hbm, slot_ref, sems.at[1]),
        pltpu.make_async_copy(len_hbm, len_ref, sems.at[3]),
        pltpu.make_async_copy(x_hbm.at[:, pl.ds(start, width)], x_ref, sems.at[2]),
    ]
    for copy in copies:
        copy.start()
    for copy in copies[:3]:
        copy.wait()
    first = lax.axis_index("wide") * rows
    holder = scalars(lambda r: slot_ref[tenant_ref[first + r]], rows)
    sublane, lane = iota((rows, rows), 0), iota((rows, rows), 1)
    holder_col = jnp.sum(jnp.where(sublane == lane, holder, 0), axis=1, keepdims=True)
    earlier = (holder_col == holder) & (sublane < lane)
    place = jnp.sum(earlier.astype(jnp.int32), axis=0, keepdims=True)
    dest = (holder ^ here) * capacity + place
    table_ref[0:1] = dest
    table_ref[1:2] = scalars(lambda r: len_ref[r], rows)
    chosen = (iota((slots, rows), 0) == dest).astype(F32).astype(BF16)
    copies[3].wait()
    store_blocks(packed_refs, dot(chosen, x_ref[...]))


def down_body(ret_refs, down_ref, out_ref):
    rows = joined(ret_refs)
    width = rows.shape[1]
    start = pl.multiple_of(lax.axis_index("tp") * width, width)
    out_ref[...] = dot_t(rows, down_ref[0, :, pl.ds(start, width)])


def output_down_body(ret_refs, down_ref, out_ref):
    out_ref[...] = dot_t(joined(ret_refs), down_ref[0])


def up_body(group, mine_ref, other_ref, uq_ref, ukv_ref, *out_refs):
    rank = uq_ref.shape[1]
    total = (mine_ref[...] + other_ref[...]).astype(BF16)
    q_width = uq_ref.shape[2]
    width = ukv_ref.shape[3]
    store_blocks(out_refs, dot(total[:, :rank], uq_ref[0]), slice(0, q_width))
    for i in range(2):
        store_blocks(
            out_refs,
            dot(total[:, (i + 1) * rank : (i + 2) * rank], ukv_ref[0, i]),
            slice(q_width + i * width, q_width + (i + 1) * width),
        )


def prep_body(group, table_ref, bias_ref, take_ref, send_ref, home_ref):
    lines = bias_ref.shape[0]
    rows, slots = home_ref.shape
    shift = group.bit_length() - 1
    dest_row, len_row = table_ref[0:1], table_ref[1:2]
    mine = (iota((lines, rows), 0) >> shift) == iota((lines, rows), 1)
    len_line = jnp.sum(jnp.where(mine, len_row, 0), axis=1, keepdims=True)
    eye = iota((rows, rows), 0) == iota((rows, rows), 1)
    dest_col = jnp.sum(jnp.where(eye, dest_row, 0), axis=1, keepdims=True)
    bias_ref[...] = jnp.where(iota(bias_ref.shape, 1) < len_line, 0.0, -jnp.inf)
    at_home = iota((rows, slots), 1) == dest_col
    take_ref[...] = jnp.where(at_home, ADAPTER_SCALE, 0.0).astype(BF16)
    send_ref[...] = (iota((slots, rows), 0) == dest_row).astype(F32).astype(BF16)
    home_ref[...] = at_home.astype(F32).astype(BF16)


def attend_body(
    group, ret_refs, k_ref, v_ref, pq_ref, pk_ref, pv_ref, bias_ref, take_ref, send_ref, home_ref, *refs,
):
    packed_refs, (context_ref, term_ref, line_ref) = refs[:-3], refs[-3:]
    rows, heads, cache_size, head_dim = k_ref.shape
    take, send = take_ref[...], send_ref[...]
    bias = bias_ref[...]
    scale = head_dim ** (-0.5)
    k_base = heads * group * head_dim
    v_base = k_base + heads * head_dim
    term_ref[...] = dot(take, joined(ret_refs))
    for base, plain in ((0, pq_ref), (k_base, pk_ref), (v_base, pv_ref)):
        term_ref[:, base : base + plain.shape[1]] += plain[...].astype(F32)

    def lines_of(slot, part):
        for h in range(group):
            line_ref[slot, pl.ds(h, rows, stride=group), :] = part(h)
        return line_ref[slot]

    def beside(value, r, side):
        lines = value[r * group : (r + 1) * group]
        pair = [jnp.zeros_like(lines)] * 2
        pair[side] = lines
        return jnp.concatenate(pair, axis=1)

    for g in range(heads):
        slot = 4 * (g % 2)
        columns = slice(g * group * head_dim, (g + 1) * group * head_dim)
        query_rows = term_ref[:, columns]
        query = lines_of(slot, lambda h: query_rows[:, h * head_dim : (h + 1) * head_dim])
        query = query.astype(BF16).astype(F32)
        key_columns = slice(g * head_dim, (g + 1) * head_dim)
        new_key, new_value = (
            term_ref[:, base + g * head_dim : base + (g + 1) * head_dim].astype(BF16).astype(F32)
            for base in (k_base, v_base)
        )
        new_key = lines_of(slot + 1, lambda h: new_key)
        new_value = lines_of(slot + 2, lambda h: new_value)
        own = jnp.sum(query * new_key, axis=1, keepdims=True) * scale
        score = jnp.concatenate(
            [
                dot_t(
                    jnp.concatenate([beside(query, r, 0), beside(query, r + 1, 1)], axis=0).astype(BF16),
                    jnp.concatenate([k_ref[r, g], k_ref[r + 1, g]], axis=1),
                )
                for r in range(0, rows, 2)
            ],
            axis=0,
        )
        score = score * scale + bias
        highest = jnp.maximum(jnp.max(score, axis=1, keepdims=True), own)
        raised = jnp.exp(score - highest)
        own_raised = jnp.exp(own - highest)
        inverse = 1.0 / (jnp.sum(raised, axis=1, keepdims=True) + own_raised)
        weight = raised * inverse
        own_weight = (own_raised * inverse).astype(BF16).astype(F32)
        attended = jnp.concatenate(
            [dot(weight[r * group : (r + 1) * group].astype(BF16), v_ref[r, g]) for r in range(rows)], axis=0
        )
        line_ref[slot + 3] = attended + own_weight * new_value
        context = jnp.concatenate(
            [line_ref[slot + 3, pl.ds(h, rows, stride=group), :] for h in range(group)], axis=1
        ).astype(BF16)
        context_ref[:, columns] = context
    store_blocks(packed_refs, dot(send, context_ref[...]))


def output_up_body(mine_ref, other_ref, uo_ref, *out_refs):
    total = (mine_ref[...] + other_ref[...]).astype(BF16)
    store_blocks(out_refs, ADAPTER_SCALE * dot(total, uo_ref[0]))


def unpack_body(home_ref, ret_refs, out_hbm, out_ref, sems):
    rows, width = out_ref.shape
    home = home_ref[...]
    returned = joined(ret_refs)
    parts = sems.shape[0]
    part = width // parts
    leaving = []
    for i in range(parts):
        columns = slice(i * part, (i + 1) * part)
        out_ref[:, columns] = dot(home, returned[:, columns]).astype(BF16)
        copy = pltpu.make_async_copy(out_ref.at[:, columns], out_hbm.at[:, columns], sems.at[i])
        copy.start()
        leaving.append(copy)
    for copy in leaving:
        copy.wait()


def exchange(blocks, wide_count):
    if len(blocks) == 1:
        slots, width = blocks[0].shape
        moved = lax.all_to_all(
            blocks[0].reshape(wide_count, slots // wide_count, width), "wide", split_axis=0, concat_axis=0, tiled=True
        )
        return (moved.reshape(slots, width),)
    moved = [
        lax.ppermute(block, "wide", [(k, k ^ d) for k in range(wide_count)])
        for d, block in zip(distances(wide_count), blocks[:-1])
    ]
    return (*moved, blocks[-1])


def other_core(value):
    return lax.ppermute(value, "tp", [(0, 1), (1, 0)])


def shards(
    normed_layer_input,
    plain_query_rows,
    plain_key_rows,
    plain_value_rows,
    cached_key_rows,
    cached_value_rows,
    live_cache_length,
    tenant,
    slot_of_adapter,
    stacked_down_weight,
    query_up_weight,
    key_value_up_weight,
    output_down_weight,
    output_up_weight,
):
    wide_count = lax.axis_size("wide")
    rows, features = normed_layer_input.shape
    half = features // lax.axis_size("tp")
    capacity = max(2, 2 * rows // wide_count)
    slots = wide_count * capacity
    kv_heads, cache_size, head_dim = cached_key_rows.shape[1:]
    query_width = plain_query_rows.shape[1]
    group = query_width // head_dim // kv_heads
    lines = rows * group
    by_distance = wide_count <= 8 and wide_count & (wide_count - 1) == 0
    count = wide_count if by_distance else 1
    struct = jax.ShapeDtypeStruct

    def blocks_of(width):
        return [struct((slots // count, width), BF16)] * count


    table, *packed = call(
        functools.partial(pack_body, capacity, by_distance),
        (struct((2, rows), jnp.int32), *blocks_of(half)),
        [HBM] * 4,
        scratch=[
            pltpu.SMEM(tenant.shape, jnp.int32),
            pltpu.SMEM(slot_of_adapter.shape, jnp.int32),
            pltpu.SMEM((rows,), jnp.int32),
            pltpu.VMEM((rows, half), BF16),
            DMA((4,)),
        ],
        flops=10**9,
        moved=40000000,
    )(tenant, slot_of_adapter, live_cache_length, normed_layer_input)
    received = exchange(packed, wide_count)
    prepared = (
        struct((lines, cache_size), F32),
        struct((rows, slots), BF16),
        struct((slots, rows), BF16),
        struct((rows, slots), BF16),
    )
    prepared = call(
        functools.partial(prep_body, group), prepared, [VMEM], flops=10**9, moved=20000000, limit=16
    )(table)
    received, prepared = lax.optimization_barrier((received, prepared))
    rank_part = call(
        down_body, struct((slots, stacked_down_weight.shape[1]), F32), [(VMEM,) * count, VMEM], moved=4000000, limit=16
    )(received, stacked_down_weight)
    rank_other = other_core(rank_part)
    home = prepared[3]
    terms = call(
        functools.partial(up_body, group),
        blocks_of(kv_heads * (group + 2) * head_dim),
        [VMEM] * 4,
        moved=20000000,
        flops=10**9,
        limit=16,
    )(rank_part, rank_other, query_up_weight, key_value_up_weight)
    returned = exchange(terms, wide_count)
    *outgoing, context = call(
        functools.partial(attend_body, group),
        [*blocks_of(query_width), struct((rows, query_width), BF16)],
        [(VMEM,) * count] + [VMEM] * (5 + len(prepared)),
        scratch=[
            pltpu.VMEM((rows, kv_heads * (group + 2) * head_dim), F32),
            pltpu.VMEM((8, lines, head_dim), F32),
        ],
        moved=8000000,
        limit=16,
    )(
        returned, cached_key_rows, cached_value_rows, plain_query_rows, plain_key_rows, plain_value_rows, *prepared
    )
    arrived = exchange(outgoing, wide_count)
    rank_o = call(
        output_down_body, struct((slots, output_down_weight.shape[1]), F32), [(VMEM,) * count, VMEM], moved=4000000, limit=16
    )(arrived, output_down_weight)
    out_terms = call(
        output_up_body, blocks_of(query_width), [VMEM] * 3, moved=1200000, limit=16
    )(rank_o, other_core(rank_o), output_up_weight)
    adapter_output_term = call(
        unpack_body, struct((rows, query_width), BF16), [VMEM, (VMEM,) * count], HBM,
        scratch=[pltpu.VMEM((rows, query_width), BF16), DMA((4,))], moved=1000000, limit=16,
    )(home, exchange(out_terms, wide_count))
    return context, adapter_output_term


def solution(mesh):
    return jax.shard_map(
        shards,
        mesh=mesh,
        in_specs=(
            P(("groups", "wide"), None),
            P(("groups", "wide"), "tp"),
            P(("groups", "wide"), "tp"),
            P(("groups", "wide"), "tp"),
            P(("groups", "wide"), "tp", None, None),
            P(("groups", "wide"), "tp", None, None),
            P(("groups", "wide")),
            P("groups"),
            P("groups"),
            P("wide", None, None),
            P("wide", None, "tp"),
            P("wide", None, None, "tp"),
            P("wide", None, "tp"),
            P("wide", None, "tp"),
        ),
        out_specs=(P(("groups", "wide"), "tp"), P(("groups", "wide"), "tp")),
        check_vma=False,
    )
```

```python
import functools

import jax
import jax.numpy as jnp
from jax import lax
from jax.experimental import pallas as pl
from jax.experimental.pallas import tpu as pltpu
from jax.sharding import PartitionSpec as P

ADAPTER_SCALE = 0.5
SEND_ORDER = (7, 2, 5, 4, 3, 6, 1)
F32 = jnp.float32
BF16 = jnp.bfloat16
VMEM = pl.BlockSpec(memory_space=pltpu.VMEM)
SMEM = pl.BlockSpec(memory_space=pltpu.SMEM)
HBM = pl.BlockSpec(memory_space=pltpu.HBM)
DMA = pltpu.SemaphoreType.DMA


def call(body, out_shape, in_specs, out_specs=None, scratch=(), flops=0, moved=0, limit=58):
    return pl.pallas_call(
        body,
        out_shape=out_shape,
        in_specs=in_specs,
        out_specs=jax.tree.map(lambda _: VMEM, out_shape) if out_specs is None else out_specs,
        scratch_shapes=scratch,
        cost_estimate=pl.CostEstimate(flops=flops, bytes_accessed=moved, transcendentals=0),
        compiler_params=pltpu.CompilerParams(vmem_limit_bytes=limit * 1024 * 1024),
    )


def iota(shape, dim):
    return lax.broadcasted_iota(jnp.int32, shape, dim)


def dot(a, b):
    return lax.dot_general(a, b, (((1,), (0,)), ((), ())), preferred_element_type=F32)


def dot_t(a, b):
    return lax.dot_general(a, b, (((1,), (1,)), ((), ())), preferred_element_type=F32)


def scalars(read, rows):
    lane = iota((1, rows), 1)
    row = jnp.zeros((1, rows), jnp.int32)
    for r in range(rows):
        row = jnp.where(lane == r, read(r), row)
    return row


def distances(count):
    return [d for d in SEND_ORDER if d < count] + [0]


def joined(refs):
    if len(refs) == 1:
        return refs[0][...]
    listed = sorted(zip(distances(len(refs)), refs), key=lambda pair: pair[0])
    return jnp.concatenate([ref[...].astype(F32) for _, ref in listed], axis=0).astype(BF16)


def store_blocks(refs, value, columns=slice(None)):
    rows = value.shape[0] // len(refs)
    for d, ref in zip(distances(len(refs)), refs):
        ref[:, columns] = value[d * rows : (d + 1) * rows].astype(BF16)


def pack_body(capacity, by_distance, tenant_hbm, slot_hbm, len_hbm, x_hbm, table_ref, *refs):
    packed_refs, (tenant_ref, slot_ref, len_ref, x_ref, sems) = refs[:-5], refs[-5:]
    slots = sum(ref.shape[0] for ref in packed_refs)
    rows, width = x_ref.shape
    here = lax.axis_index("wide") if by_distance else 0
    start = pl.multiple_of(lax.axis_index("tp") * width, width)
    copies = [
        pltpu.make_async_copy(tenant_hbm, tenant_ref, sems.at[0]),
        pltpu.make_async_copy(slot_hbm, slot_ref, sems.at[1]),
        pltpu.make_async_copy(len_hbm, len_ref, sems.at[3]),
        pltpu.make_async_copy(x_hbm.at[:, pl.ds(start, width)], x_ref, sems.at[2]),
    ]
    for copy in copies:
        copy.start()
    for copy in copies[:3]:
        copy.wait()
    first = lax.axis_index("wide") * rows
    holder = scalars(lambda r: slot_ref[tenant_ref[first + r]], rows)
    sublane, lane = iota((rows, rows), 0), iota((rows, rows), 1)
    holder_col = jnp.sum(jnp.where(sublane == lane, holder, 0), axis=1, keepdims=True)
    earlier = (holder_col == holder) & (sublane < lane)
    place = jnp.sum(earlier.astype(jnp.int32), axis=0, keepdims=True)
    dest = (holder ^ here) * capacity + place
    table_ref[0:1] = dest
    table_ref[1:2] = scalars(lambda r: len_ref[r], rows)
    chosen = (iota((slots, rows), 0) == dest).astype(F32).astype(BF16)
    copies[3].wait()
    store_blocks(packed_refs, dot(chosen, x_ref[...]))


def down_body(ret_refs, down_ref, out_ref):
    rows = joined(ret_refs)
    width = rows.shape[1]
    start = pl.multiple_of(lax.axis_index("tp") * width, width)
    out_ref[...] = dot_t(rows, down_ref[0, :, pl.ds(start, width)])


def output_down_body(ret_refs, down_ref, out_ref):
    out_ref[...] = dot_t(joined(ret_refs), down_ref[0])


def up_body(group, mine_ref, other_ref, uq_ref, ukv_ref, *out_refs):
    rank = uq_ref.shape[1]
    total = (mine_ref[...] + other_ref[...]).astype(BF16)
    q_width = uq_ref.shape[2]
    width = ukv_ref.shape[3]
    store_blocks(out_refs, dot(total[:, :rank], uq_ref[0]), slice(0, q_width))
    for i in range(2):
        store_blocks(
            out_refs,
            dot(total[:, (i + 1) * rank : (i + 2) * rank], ukv_ref[0, i]),
            slice(q_width + i * width, q_width + (i + 1) * width),
        )


def prep_body(group, table_ref, bias_ref, take_ref, send_ref, home_ref):
    lines = bias_ref.shape[0]
    rows, slots = home_ref.shape
    shift = group.bit_length() - 1
    dest_row, len_row = table_ref[0:1], table_ref[1:2]
    mine = (iota((lines, rows), 0) >> shift) == iota((lines, rows), 1)
    len_line = jnp.sum(jnp.where(mine, len_row, 0), axis=1, keepdims=True)
    eye = iota((rows, rows), 0) == iota((rows, rows), 1)
    dest_col = jnp.sum(jnp.where(eye, dest_row, 0), axis=1, keepdims=True)
    bias_ref[...] = jnp.where(iota(bias_ref.shape, 1) < len_line, 0.0, -jnp.inf)
    at_home = iota((rows, slots), 1) == dest_col
    take_ref[...] = jnp.where(at_home, ADAPTER_SCALE, 0.0).astype(BF16)
    send_ref[...] = (iota((slots, rows), 0) == dest_row).astype(F32).astype(BF16)
    home_ref[...] = at_home.astype(F32).astype(BF16)


def attend_body(
    group, ret_refs, k_ref, v_ref, pq_ref, pk_ref, pv_ref, bias_ref, take_ref, send_ref, home_ref, *refs,
):
    packed_refs, (context_ref, term_ref, line_ref) = refs[:-3], refs[-3:]
    rows, heads, cache_size, head_dim = k_ref.shape
    take, send = take_ref[...], send_ref[...]
    bias = bias_ref[...]
    scale = head_dim ** (-0.5)
    k_base = heads * group * head_dim
    v_base = k_base + heads * head_dim
    term_ref[...] = dot(take, joined(ret_refs))
    for base, plain in ((0, pq_ref), (k_base, pk_ref), (v_base, pv_ref)):
        term_ref[:, base : base + plain.shape[1]] += plain[...].astype(F32)

    def lines_of(slot, part):
        for h in range(group):
            line_ref[slot, pl.ds(h, rows, stride=group), :] = part(h)
        return line_ref[slot]

    def beside(value, r, side):
        lines = value[r * group : (r + 1) * group]
        pair = [jnp.zeros_like(lines)] * 2
        pair[side] = lines
        return jnp.concatenate(pair, axis=1)

    for g in range(heads):
        slot = 4 * (g % 2)
        columns = slice(g * group * head_dim, (g + 1) * group * head_dim)
        query_rows = term_ref[:, columns]
        query = lines_of(slot, lambda h: query_rows[:, h * head_dim : (h + 1) * head_dim])
        query = query.astype(BF16).astype(F32)
        key_columns = slice(g * head_dim, (g + 1) * head_dim)
        new_key, new_value = (
            term_ref[:, base + g * head_dim : base + (g + 1) * head_dim].astype(BF16).astype(F32)
            for base in (k_base, v_base)
        )
        new_key = lines_of(slot + 1, lambda h: new_key)
        new_value = lines_of(slot + 2, lambda h: new_value)
        own = jnp.sum(query * new_key, axis=1, keepdims=True) * scale
        score = jnp.concatenate(
            [
                dot_t(
                    jnp.concatenate([beside(query, r, 0), beside(query, r + 1, 1)], axis=0).astype(BF16),
                    jnp.concatenate([k_ref[r, g], k_ref[r + 1, g]], axis=1),
                )
                for r in range(0, rows, 2)
            ],
            axis=0,
        )
        score = score * scale + bias
        highest = jnp.maximum(jnp.max(score, axis=1, keepdims=True), own)
        raised = jnp.exp(score - highest)
        own_raised = jnp.exp(own - highest)
        inverse = 1.0 / (jnp.sum(raised, axis=1, keepdims=True) + own_raised)
        weight = raised * inverse
        own_weight = (own_raised * inverse).astype(BF16).astype(F32)
        attended = jnp.concatenate(
            [dot(weight[r * group : (r + 1) * group].astype(BF16), v_ref[r, g]) for r in range(rows)], axis=0
        )
        line_ref[slot + 3] = attended + own_weight * new_value
        context = jnp.concatenate(
            [line_ref[slot + 3, pl.ds(h, rows, stride=group), :] for h in range(group)], axis=1
        ).astype(BF16)
        context_ref[:, columns] = context
    store_blocks(packed_refs, dot(send, context_ref[...]))


def output_up_body(mine_ref, other_ref, uo_ref, *out_refs):
    total = (mine_ref[...] + other_ref[...]).astype(BF16)
    store_blocks(out_refs, ADAPTER_SCALE * dot(total, uo_ref[0]))


def unpack_body(home_ref, ret_refs, out_hbm, out_ref, sems):
    rows, width = out_ref.shape
    home = home_ref[...]
    returned = joined(ret_refs)
    parts = sems.shape[0]
    part = width // parts
    leaving = []
    for i in range(parts):
        columns = slice(i * part, (i + 1) * part)
        out_ref[:, columns] = dot(home, returned[:, columns]).astype(BF16)
        copy = pltpu.make_async_copy(out_ref.at[:, columns], out_hbm.at[:, columns], sems.at[i])
        copy.start()
        leaving.append(copy)
    for copy in leaving:
        copy.wait()


def exchange(blocks, wide_count):
    if len(blocks) == 1:
        slots, width = blocks[0].shape
        moved = lax.all_to_all(
            blocks[0].reshape(wide_count, slots // wide_count, width), "wide", split_axis=0, concat_axis=0, tiled=True
        )
        return (moved.reshape(slots, width),)
    moved = [
        lax.ppermute(block, "wide", [(k, k ^ d) for k in range(wide_count)])
        for d, block in zip(distances(wide_count), blocks[:-1])
    ]
    return (*moved, blocks[-1])


def other_core(value):
    return lax.ppermute(value, "tp", [(0, 1), (1, 0)])


def shards(
    normed_layer_input,
    plain_query_rows,
    plain_key_rows,
    plain_value_rows,
    cached_key_rows,
    cached_value_rows,
    live_cache_length,
    tenant,
    slot_of_adapter,
    stacked_down_weight,
    query_up_weight,
    key_value_up_weight,
    output_down_weight,
    output_up_weight,
):
    wide_count = lax.axis_size("wide")
    rows, features = normed_layer_input.shape
    half = features // lax.axis_size("tp")
    capacity = max(2, 2 * rows // wide_count)
    slots = wide_count * capacity
    kv_heads, cache_size, head_dim = cached_key_rows.shape[1:]
    query_width = plain_query_rows.shape[1]
    group = query_width // head_dim // kv_heads
    lines = rows * group
    by_distance = wide_count <= 8 and wide_count & (wide_count - 1) == 0
    count = wide_count if by_distance else 1
    struct = jax.ShapeDtypeStruct

    def blocks_of(width):
        return [struct((slots // count, width), BF16)] * count


    table, *packed = call(
        functools.partial(pack_body, capacity, by_distance),
        (struct((2, rows), jnp.int32), *blocks_of(half)),
        [HBM] * 4,
        scratch=[
            pltpu.SMEM(tenant.shape, jnp.int32),
            pltpu.SMEM(slot_of_adapter.shape, jnp.int32),
            pltpu.SMEM((rows,), jnp.int32),
            pltpu.VMEM((rows, half), BF16),
            DMA((4,)),
        ],
        flops=10**9,
        moved=40000000,
    )(tenant, slot_of_adapter, live_cache_length, normed_layer_input)
    received = exchange(packed, wide_count)
    prepared = (
        struct((lines, cache_size), F32),
        struct((rows, slots), BF16),
        struct((slots, rows), BF16),
        struct((rows, slots), BF16),
    )
    prepared = call(
        functools.partial(prep_body, group), prepared, [VMEM], flops=10**9, moved=20000000, limit=16
    )(table)
    received, prepared = lax.optimization_barrier((received, prepared))
    rank_part = call(
        down_body, struct((slots, stacked_down_weight.shape[1]), F32), [(VMEM,) * count, VMEM], moved=4000000, limit=16
    )(received, stacked_down_weight)
    rank_other = other_core(rank_part)
    home = prepared[3]
    terms = call(
        functools.partial(up_body, group),
        blocks_of(kv_heads * (group + 2) * head_dim),
        [VMEM] * 4,
        moved=20000000,
        flops=10**9,
        limit=16,
    )(rank_part, rank_other, query_up_weight, key_value_up_weight)
    returned = exchange(terms, wide_count)
    *outgoing, context = call(
        functools.partial(attend_body, group),
        [*blocks_of(query_width), struct((rows, query_width), BF16)],
        [(VMEM,) * count] + [VMEM] * (5 + len(prepared)),
        scratch=[
            pltpu.VMEM((rows, kv_heads * (group + 2) * head_dim), F32),
            pltpu.VMEM((8, lines, head_dim), F32),
        ],
        moved=8000000,
        limit=16,
    )(
        returned, cached_key_rows, cached_value_rows, plain_query_rows, plain_key_rows, plain_value_rows, *prepared
    )
    arrived = exchange(outgoing, wide_count)
    rank_o = call(
        output_down_body, struct((slots, output_down_weight.shape[1]), F32), [(VMEM,) * count, VMEM], moved=4000000, limit=16
    )(arrived, output_down_weight)
    out_terms = call(
        output_up_body, blocks_of(query_width), [VMEM] * 3, moved=1200000, limit=16
    )(rank_o, other_core(rank_o), output_up_weight)
    adapter_output_term = call(
        unpack_body, struct((rows, query_width), BF16), [VMEM, (VMEM,) * count], HBM,
        scratch=[pltpu.VMEM((rows, query_width), BF16), DMA((4,))], moved=1000000, limit=16,
    )(home, exchange(out_terms, wide_count))
    return context, adapter_output_term


def solution(mesh):
    return jax.shard_map(
        shards,
        mesh=mesh,
        in_specs=(
            P(("groups", "wide"), None),
            P(("groups", "wide"), "tp"),
            P(("groups", "wide"), "tp"),
            P(("groups", "wide"), "tp"),
            P(("groups", "wide"), "tp", None, None),
            P(("groups", "wide"), "tp", None, None),
            P(("groups", "wide")),
            P("groups"),
            P("groups"),
            P("wide", None, None),
            P("wide", None, "tp"),
            P("wide", None, None, "tp"),
            P("wide", None, "tp"),
            P("wide", None, "tp"),
        ),
        out_specs=(P(("groups", "wide"), "tp"), P(("groups", "wide"), "tp")),
        check_vma=False,
    )
```

```python
import functools

import jax
import jax.numpy as jnp
from jax import lax
from jax.experimental import pallas as pl
from jax.experimental.pallas import tpu as pltpu
from jax.sharding import PartitionSpec as P

ADAPTER_SCALE = 0.5
SEND_ORDER = (7, 2, 5, 4, 3, 6, 1)
F32 = jnp.float32
BF16 = jnp.bfloat16
VMEM = pl.BlockSpec(memory_space=pltpu.VMEM)
SMEM = pl.BlockSpec(memory_space=pltpu.SMEM)
HBM = pl.BlockSpec(memory_space=pltpu.HBM)
DMA = pltpu.SemaphoreType.DMA


def call(body, out_shape, in_specs, out_specs=None, scratch=(), flops=0, moved=0, limit=58):
    return pl.pallas_call(
        body,
        out_shape=out_shape,
        in_specs=in_specs,
        out_specs=jax.tree.map(lambda _: VMEM, out_shape) if out_specs is None else out_specs,
        scratch_shapes=scratch,
        cost_estimate=pl.CostEstimate(flops=flops, bytes_accessed=moved, transcendentals=0),
        compiler_params=pltpu.CompilerParams(vmem_limit_bytes=limit * 1024 * 1024),
    )


def iota(shape, dim):
    return lax.broadcasted_iota(jnp.int32, shape, dim)


def dot(a, b):
    return lax.dot_general(a, b, (((1,), (0,)), ((), ())), preferred_element_type=F32)


def dot_t(a, b):
    return lax.dot_general(a, b, (((1,), (1,)), ((), ())), preferred_element_type=F32)


def scalars(read, rows):
    lane = iota((1, rows), 1)
    row = jnp.zeros((1, rows), jnp.int32)
    for r in range(rows):
        row = jnp.where(lane == r, read(r), row)
    return row


def distances(count):
    return [d for d in SEND_ORDER if d < count] + [0]


def joined(refs):
    if len(refs) == 1:
        return refs[0][...]
    listed = sorted(zip(distances(len(refs)), refs), key=lambda pair: pair[0])
    return jnp.concatenate([ref[...].astype(F32) for _, ref in listed], axis=0).astype(BF16)


def store_blocks(refs, value, columns=slice(None)):
    rows = value.shape[0] // len(refs)
    for d, ref in zip(distances(len(refs)), refs):
        ref[:, columns] = value[d * rows : (d + 1) * rows].astype(BF16)


def pack_body(capacity, by_distance, tenant_hbm, slot_hbm, len_hbm, x_hbm, table_ref, *refs):
    packed_refs, (tenant_ref, slot_ref, len_ref, x_ref, sems) = refs[:-5], refs[-5:]
    slots = sum(ref.shape[0] for ref in packed_refs)
    rows, width = x_ref.shape
    here = lax.axis_index("wide") if by_distance else 0
    start = pl.multiple_of(lax.axis_index("tp") * width, width)
    copies = [
        pltpu.make_async_copy(tenant_hbm, tenant_ref, sems.at[0]),
        pltpu.make_async_copy(slot_hbm, slot_ref, sems.at[1]),
        pltpu.make_async_copy(len_hbm, len_ref, sems.at[3]),
        pltpu.make_async_copy(x_hbm.at[:, pl.ds(start, width)], x_ref, sems.at[2]),
    ]
    for copy in copies:
        copy.start()
    for copy in copies[:3]:
        copy.wait()
    first = lax.axis_index("wide") * rows
    holder = scalars(lambda r: slot_ref[tenant_ref[first + r]], rows)
    sublane, lane = iota((rows, rows), 0), iota((rows, rows), 1)
    holder_col = jnp.sum(jnp.where(sublane == lane, holder, 0), axis=1, keepdims=True)
    earlier = (holder_col == holder) & (sublane < lane)
    place = jnp.sum(earlier.astype(jnp.int32), axis=0, keepdims=True)
    dest = (holder ^ here) * capacity + place
    table_ref[0:1] = dest
    table_ref[1:2] = scalars(lambda r: len_ref[r], rows)
    chosen = (iota((slots, rows), 0) == dest).astype(F32).astype(BF16)
    copies[3].wait()
    store_blocks(packed_refs, dot(chosen, x_ref[...]))


def down_body(ret_refs, down_ref, out_ref):
    rows = joined(ret_refs)
    width = rows.shape[1]
    start = pl.multiple_of(lax.axis_index("tp") * width, width)
    out_ref[...] = dot_t(rows, down_ref[0, :, pl.ds(start, width)])


def output_down_body(ret_refs, down_ref, out_ref):
    out_ref[...] = dot_t(joined(ret_refs), down_ref[0])


def up_body(group, mine_ref, other_ref, uq_ref, ukv_ref, *out_refs):
    rank = uq_ref.shape[1]
    total = (mine_ref[...] + other_ref[...]).astype(BF16)
    q_width = uq_ref.shape[2]
    width = ukv_ref.shape[3]
    store_blocks(out_refs, dot(total[:, :rank], uq_ref[0]), slice(0, q_width))
    for i in range(2):
        store_blocks(
            out_refs,
            dot(total[:, (i + 1) * rank : (i + 2) * rank], ukv_ref[0, i]),
            slice(q_width + i * width, q_width + (i + 1) * width),
        )


def prep_body(group, table_ref, bias_ref, take_ref, send_ref, home_ref):
    lines = bias_ref.shape[0]
    rows, slots = home_ref.shape
    shift = group.bit_length() - 1
    dest_row, len_row = table_ref[0:1], table_ref[1:2]
    mine = (iota((lines, rows), 0) >> shift) == iota((lines, rows), 1)
    len_line = jnp.sum(jnp.where(mine, len_row, 0), axis=1, keepdims=True)
    eye = iota((rows, rows), 0) == iota((rows, rows), 1)
    dest_col = jnp.sum(jnp.where(eye, dest_row, 0), axis=1, keepdims=True)
    bias_ref[...] = jnp.where(iota(bias_ref.shape, 1) < len_line, 0.0, -jnp.inf)
    at_home = iota((rows, slots), 1) == dest_col
    take_ref[...] = jnp.where(at_home, ADAPTER_SCALE, 0.0).astype(BF16)
    send_ref[...] = (iota((slots, rows), 0) == dest_row).astype(F32).astype(BF16)
    home_ref[...] = at_home.astype(F32).astype(BF16)


def attend_body(
    group, ret_refs, k_ref, v_ref, pq_ref, pk_ref, pv_ref, bias_ref, take_ref, send_ref, home_ref, *refs,
):
    packed_refs, (context_ref, term_ref, line_ref) = refs[:-3], refs[-3:]
    rows, heads, cache_size, head_dim = k_ref.shape
    take, send = take_ref[...], send_ref[...]
    bias = bias_ref[...]
    scale = head_dim ** (-0.5)
    k_base = heads * group * head_dim
    v_base = k_base + heads * head_dim
    term_ref[...] = dot(take, joined(ret_refs))
    for base, plain in ((0, pq_ref), (k_base, pk_ref), (v_base, pv_ref)):
        term_ref[:, base : base + plain.shape[1]] += plain[...].astype(F32)

    def lines_of(slot, part):
        for h in range(group):
            line_ref[slot, pl.ds(h, rows, stride=group), :] = part(h)
        return line_ref[slot]

    def beside(value, r, side):
        lines = value[r * group : (r + 1) * group]
        pair = [jnp.zeros_like(lines)] * 2
        pair[side] = lines
        return jnp.concatenate(pair, axis=1)

    held = []
    for g in range(heads):
        slot = 4 * g
        columns = slice(g * group * head_dim, (g + 1) * group * head_dim)
        query_rows = term_ref[:, columns]
        query = lines_of(slot, lambda h: query_rows[:, h * head_dim : (h + 1) * head_dim])
        query = query.astype(BF16).astype(F32)
        key_columns = slice(g * head_dim, (g + 1) * head_dim)
        new_key, new_value = (
            term_ref[:, base + g * head_dim : base + (g + 1) * head_dim].astype(BF16).astype(F32)
            for base in (k_base, v_base)
        )
        new_key = lines_of(slot + 1, lambda h: new_key)
        new_value = lines_of(slot + 2, lambda h: new_value)
        own = jnp.sum(query * new_key, axis=1, keepdims=True) * scale
        score = jnp.concatenate(
            [
                dot_t(
                    jnp.concatenate([beside(query, r, 0), beside(query, r + 1, 1)], axis=0).astype(BF16),
                    jnp.concatenate([k_ref[r, g], k_ref[r + 1, g]], axis=1),
                )
                for r in range(0, rows, 2)
            ],
            axis=0,
        )
        held.append((own, score))
    for g in range(heads):
        slot = 4 * g
        columns = slice(g * group * head_dim, (g + 1) * group * head_dim)
        own, score = held[g]
        new_value = line_ref[slot + 2]
        score = score * scale + bias
        highest = jnp.maximum(jnp.max(score, axis=1, keepdims=True), own)
        raised = jnp.exp(score - highest)
        own_raised = jnp.exp(own - highest)
        inverse = 1.0 / (jnp.sum(raised, axis=1, keepdims=True) + own_raised)
        weight = raised * inverse
        own_weight = (own_raised * inverse).astype(BF16).astype(F32)
        attended = jnp.concatenate(
            [dot(weight[r * group : (r + 1) * group].astype(BF16), v_ref[r, g]) for r in range(rows)], axis=0
        )
        line_ref[slot + 3] = attended + own_weight * new_value
        context = jnp.concatenate(
            [line_ref[slot + 3, pl.ds(h, rows, stride=group), :] for h in range(group)], axis=1
        ).astype(BF16)
        context_ref[:, columns] = context
    store_blocks(packed_refs, dot(send, context_ref[...]))


def output_up_body(mine_ref, other_ref, uo_ref, *out_refs):
    total = (mine_ref[...] + other_ref[...]).astype(BF16)
    store_blocks(out_refs, ADAPTER_SCALE * dot(total, uo_ref[0]))


def unpack_body(home_ref, ret_refs, out_hbm, out_ref, sems):
    rows, width = out_ref.shape
    home = home_ref[...]
    returned = joined(ret_refs)
    parts = sems.shape[0]
    part = width // parts
    leaving = []
    for i in range(parts):
        columns = slice(i * part, (i + 1) * part)
        out_ref[:, columns] = dot(home, returned[:, columns]).astype(BF16)
        copy = pltpu.make_async_copy(out_ref.at[:, columns], out_hbm.at[:, columns], sems.at[i])
        copy.start()
        leaving.append(copy)
    for copy in leaving:
        copy.wait()


def exchange(blocks, wide_count):
    if len(blocks) == 1:
        slots, width = blocks[0].shape
        moved = lax.all_to_all(
            blocks[0].reshape(wide_count, slots // wide_count, width), "wide", split_axis=0, concat_axis=0, tiled=True
        )
        return (moved.reshape(slots, width),)
    moved = [
        lax.ppermute(block, "wide", [(k, k ^ d) for k in range(wide_count)])
        for d, block in zip(distances(wide_count), blocks[:-1])
    ]
    return (*moved, blocks[-1])


def other_core(value):
    return lax.ppermute(value, "tp", [(0, 1), (1, 0)])


def shards(
    normed_layer_input,
    plain_query_rows,
    plain_key_rows,
    plain_value_rows,
    cached_key_rows,
    cached_value_rows,
    live_cache_length,
    tenant,
    slot_of_adapter,
    stacked_down_weight,
    query_up_weight,
    key_value_up_weight,
    output_down_weight,
    output_up_weight,
):
    wide_count = lax.axis_size("wide")
    rows, features = normed_layer_input.shape
    half = features // lax.axis_size("tp")
    capacity = max(2, 2 * rows // wide_count)
    slots = wide_count * capacity
    kv_heads, cache_size, head_dim = cached_key_rows.shape[1:]
    query_width = plain_query_rows.shape[1]
    group = query_width // head_dim // kv_heads
    lines = rows * group
    by_distance = wide_count <= 8 and wide_count & (wide_count - 1) == 0
    count = wide_count if by_distance else 1
    struct = jax.ShapeDtypeStruct

    def blocks_of(width):
        return [struct((slots // count, width), BF16)] * count


    table, *packed = call(
        functools.partial(pack_body, capacity, by_distance),
        (struct((2, rows), jnp.int32), *blocks_of(half)),
        [HBM] * 4,
        scratch=[
            pltpu.SMEM(tenant.shape, jnp.int32),
            pltpu.SMEM(slot_of_adapter.shape, jnp.int32),
            pltpu.SMEM((rows,), jnp.int32),
            pltpu.VMEM((rows, half), BF16),
            DMA((4,)),
        ],
        flops=10**9,
        moved=40000000,
    )(tenant, slot_of_adapter, live_cache_length, normed_layer_input)
    received = exchange(packed, wide_count)
    prepared = (
        struct((lines, cache_size), F32),
        struct((rows, slots), BF16),
        struct((slots, rows), BF16),
        struct((rows, slots), BF16),
    )
    prepared = call(
        functools.partial(prep_body, group), prepared, [VMEM], flops=10**9, moved=20000000, limit=16
    )(table)
    received, prepared = lax.optimization_barrier((received, prepared))
    rank_part = call(
        down_body, struct((slots, stacked_down_weight.shape[1]), F32), [(VMEM,) * count, VMEM], moved=4000000, limit=16
    )(received, stacked_down_weight)
    rank_other = other_core(rank_part)
    home = prepared[3]
    terms = call(
        functools.partial(up_body, group),
        blocks_of(kv_heads * (group + 2) * head_dim),
        [VMEM] * 4,
        moved=20000000,
        flops=10**9,
        limit=16,
    )(rank_part, rank_other, query_up_weight, key_value_up_weight)
    returned = exchange(terms, wide_count)
    *outgoing, context = call(
        functools.partial(attend_body, group),
        [*blocks_of(query_width), struct((rows, query_width), BF16)],
        [(VMEM,) * count] + [VMEM] * (5 + len(prepared)),
        scratch=[
            pltpu.VMEM((rows, kv_heads * (group + 2) * head_dim), F32),
            pltpu.VMEM((4 * kv_heads, lines, head_dim), F32),
        ],
        moved=8000000,
        limit=16,
    )(
        returned, cached_key_rows, cached_value_rows, plain_query_rows, plain_key_rows, plain_value_rows, *prepared
    )
    arrived = exchange(outgoing, wide_count)
    rank_o = call(
        output_down_body, struct((slots, output_down_weight.shape[1]), F32), [(VMEM,) * count, VMEM], moved=4000000, limit=16
    )(arrived, output_down_weight)
    out_terms = call(
        output_up_body, blocks_of(query_width), [VMEM] * 3, moved=1200000, limit=16
    )(rank_o, other_core(rank_o), output_up_weight)
    adapter_output_term = call(
        unpack_body, struct((rows, query_width), BF16), [VMEM, (VMEM,) * count], HBM,
        scratch=[pltpu.VMEM((rows, query_width), BF16), DMA((4,))], moved=1000000, limit=16,
    )(home, exchange(out_terms, wide_count))
    return context, adapter_output_term


def solution(mesh):
    return jax.shard_map(
        shards,
        mesh=mesh,
        in_specs=(
            P(("groups", "wide"), None),
            P(("groups", "wide"), "tp"),
            P(("groups", "wide"), "tp"),
            P(("groups", "wide"), "tp"),
            P(("groups", "wide"), "tp", None, None),
            P(("groups", "wide"), "tp", None, None),
            P(("groups", "wide")),
            P("groups"),
            P("groups"),
            P("wide", None, None),
            P("wide", None, "tp"),
            P("wide", None, None, "tp"),
            P("wide", None, "tp"),
            P("wide", None, "tp"),
        ),
        out_specs=(P(("groups", "wide"), "tp"), P(("groups", "wide"), "tp")),
        check_vma=False,
    )
```

```python
import functools

import jax
import jax.numpy as jnp
from jax import lax
from jax.experimental import pallas as pl
from jax.experimental.pallas import tpu as pltpu
from jax.sharding import PartitionSpec as P

ADAPTER_SCALE = 0.5
SEND_ORDER = (7, 2, 5, 4, 3, 6, 1)
F32 = jnp.float32
BF16 = jnp.bfloat16
VMEM = pl.BlockSpec(memory_space=pltpu.VMEM)
SMEM = pl.BlockSpec(memory_space=pltpu.SMEM)
HBM = pl.BlockSpec(memory_space=pltpu.HBM)
DMA = pltpu.SemaphoreType.DMA


def call(body, out_shape, in_specs, out_specs=None, scratch=(), flops=0, moved=0, limit=58):
    return pl.pallas_call(
        body,
        out_shape=out_shape,
        in_specs=in_specs,
        out_specs=jax.tree.map(lambda _: VMEM, out_shape) if out_specs is None else out_specs,
        scratch_shapes=scratch,
        cost_estimate=pl.CostEstimate(flops=flops, bytes_accessed=moved, transcendentals=0),
        compiler_params=pltpu.CompilerParams(vmem_limit_bytes=limit * 1024 * 1024),
    )


def iota(shape, dim):
    return lax.broadcasted_iota(jnp.int32, shape, dim)


def dot(a, b):
    return lax.dot_general(a, b, (((1,), (0,)), ((), ())), preferred_element_type=F32)


def dot_t(a, b):
    return lax.dot_general(a, b, (((1,), (1,)), ((), ())), preferred_element_type=F32)


def scalars(read, rows):
    lane = iota((1, rows), 1)
    row = jnp.zeros((1, rows), jnp.int32)
    for r in range(rows):
        row = jnp.where(lane == r, read(r), row)
    return row


def distances(count):
    return [d for d in SEND_ORDER if d < count] + [0]


def joined(refs):
    if len(refs) == 1:
        return refs[0][...]
    listed = sorted(zip(distances(len(refs)), refs), key=lambda pair: pair[0])
    return jnp.concatenate([ref[...].astype(F32) for _, ref in listed], axis=0).astype(BF16)


def store_blocks(refs, value, columns=slice(None)):
    rows = value.shape[0] // len(refs)
    for d, ref in zip(distances(len(refs)), refs):
        ref[:, columns] = value[d * rows : (d + 1) * rows].astype(BF16)


def pack_body(capacity, by_distance, tenant_hbm, slot_hbm, len_hbm, x_hbm, table_ref, *refs):
    packed_refs, (tenant_ref, slot_ref, len_ref, x_ref, sems) = refs[:-5], refs[-5:]
    slots = sum(ref.shape[0] for ref in packed_refs)
    rows, width = x_ref.shape
    here = lax.axis_index("wide") if by_distance else 0
    start = pl.multiple_of(lax.axis_index("tp") * width, width)
    copies = [
        pltpu.make_async_copy(tenant_hbm, tenant_ref, sems.at[0]),
        pltpu.make_async_copy(slot_hbm, slot_ref, sems.at[1]),
        pltpu.make_async_copy(len_hbm, len_ref, sems.at[3]),
        pltpu.make_async_copy(x_hbm.at[:, pl.ds(start, width)], x_ref, sems.at[2]),
    ]
    for copy in copies:
        copy.start()
    for copy in copies[:3]:
        copy.wait()
    first = lax.axis_index("wide") * rows
    holder = scalars(lambda r: slot_ref[tenant_ref[first + r]], rows)
    sublane, lane = iota((rows, rows), 0), iota((rows, rows), 1)
    holder_col = jnp.sum(jnp.where(sublane == lane, holder, 0), axis=1, keepdims=True)
    earlier = (holder_col == holder) & (sublane < lane)
    place = jnp.sum(earlier.astype(jnp.int32), axis=0, keepdims=True)
    dest = (holder ^ here) * capacity + place
    table_ref[0:1] = dest
    table_ref[1:2] = scalars(lambda r: len_ref[r], rows)
    chosen = (iota((slots, rows), 0) == dest).astype(F32).astype(BF16)
    copies[3].wait()
    store_blocks(packed_refs, dot(chosen, x_ref[...]))


def down_body(ret_refs, down_ref, out_ref):
    rows = joined(ret_refs)
    width = rows.shape[1]
    start = pl.multiple_of(lax.axis_index("tp") * width, width)
    out_ref[...] = dot_t(rows, down_ref[0, :, pl.ds(start, width)])


def output_down_body(ret_refs, down_ref, out_ref):
    out_ref[...] = dot_t(joined(ret_refs), down_ref[0])


def up_body(group, mine_ref, other_ref, uq_ref, ukv_ref, *out_refs):
    rank = uq_ref.shape[1]
    total = (mine_ref[...] + other_ref[...]).astype(BF16)
    q_width = uq_ref.shape[2]
    width = ukv_ref.shape[3]
    store_blocks(out_refs, dot(total[:, :rank], uq_ref[0]), slice(0, q_width))
    for i in range(2):
        store_blocks(
            out_refs,
            dot(total[:, (i + 1) * rank : (i + 2) * rank], ukv_ref[0, i]),
            slice(q_width + i * width, q_width + (i + 1) * width),
        )


def prep_body(group, table_ref, bias_ref, take_ref, send_ref, home_ref):
    lines = bias_ref.shape[0]
    rows, slots = home_ref.shape
    shift = group.bit_length() - 1
    dest_row, len_row = table_ref[0:1], table_ref[1:2]
    mine = (iota((lines, rows), 0) >> shift) == iota((lines, rows), 1)
    len_line = jnp.sum(jnp.where(mine, len_row, 0), axis=1, keepdims=True)
    eye = iota((rows, rows), 0) == iota((rows, rows), 1)
    dest_col = jnp.sum(jnp.where(eye, dest_row, 0), axis=1, keepdims=True)
    bias_ref[...] = jnp.where(iota(bias_ref.shape, 1) < len_line, 0.0, -jnp.inf)
    at_home = iota((rows, slots), 1) == dest_col
    take_ref[...] = jnp.where(at_home, ADAPTER_SCALE, 0.0).astype(BF16)
    send_ref[...] = (iota((slots, rows), 0) == dest_row).astype(F32).astype(BF16)
    home_ref[...] = at_home.astype(F32).astype(BF16)


def attend_body(
    group, ret_refs, k_ref, v_ref, pq_ref, pk_ref, pv_ref, bias_ref, take_ref, send_ref, home_ref, *refs,
):
    packed_refs, (context_ref, term_ref, line_ref) = refs[:-3], refs[-3:]
    rows, heads, cache_size, head_dim = k_ref.shape
    take, send = take_ref[...], send_ref[...]
    bias = bias_ref[...]
    scale = head_dim ** (-0.5)
    k_base = heads * group * head_dim
    v_base = k_base + heads * head_dim
    term_ref[...] = dot(take, joined(ret_refs))
    for base, plain in ((0, pq_ref), (k_base, pk_ref), (v_base, pv_ref)):
        term_ref[:, base : base + plain.shape[1]] += plain[...].astype(F32)

    def lines_of(slot, part):
        for h in range(group):
            line_ref[slot, pl.ds(h, rows, stride=group), :] = part(h)
        return line_ref[slot]

    def beside(value, r, side):
        lines = value[r * group : (r + 1) * group]
        pair = [jnp.zeros_like(lines)] * 2
        pair[side] = lines
        return jnp.concatenate(pair, axis=1)

    held = []
    for g in range(heads):
        slot = 4 * g
        columns = slice(g * group * head_dim, (g + 1) * group * head_dim)
        query_rows = term_ref[:, columns]
        query = lines_of(slot, lambda h: query_rows[:, h * head_dim : (h + 1) * head_dim])
        query = query.astype(BF16).astype(F32)
        key_columns = slice(g * head_dim, (g + 1) * head_dim)
        new_key, new_value = (
            term_ref[:, base + g * head_dim : base + (g + 1) * head_dim].astype(BF16).astype(F32)
            for base in (k_base, v_base)
        )
        new_key = lines_of(slot + 1, lambda h: new_key)
        new_value = lines_of(slot + 2, lambda h: new_value)
        own = jnp.sum(query * new_key, axis=1, keepdims=True) * scale
        score = jnp.concatenate(
            [
                dot_t(
                    jnp.concatenate([beside(query, r, 0), beside(query, r + 1, 1)], axis=0).astype(BF16),
                    jnp.concatenate([k_ref[r, g], k_ref[r + 1, g]], axis=1),
                )
                for r in range(0, rows, 2)
            ],
            axis=0,
        )
        held.append((own, score))
    for g in range(heads):
        slot = 4 * g
        columns = slice(g * group * head_dim, (g + 1) * group * head_dim)
        own, score = held[g]
        score = score * scale + bias
        highest = jnp.maximum(jnp.max(score, axis=1, keepdims=True), own)
        raised = jnp.exp(score - highest)
        own_raised = jnp.exp(own - highest)
        inverse = 1.0 / (jnp.sum(raised, axis=1, keepdims=True) + own_raised)
        weight = raised * inverse
        own_weight = (own_raised * inverse).astype(BF16).astype(F32)
        held[g] = weight, own_weight
    for g in range(heads):
        slot = 4 * g
        columns = slice(g * group * head_dim, (g + 1) * group * head_dim)
        weight, own_weight = held[g]
        new_value = line_ref[slot + 2]
        attended = jnp.concatenate(
            [dot(weight[r * group : (r + 1) * group].astype(BF16), v_ref[r, g]) for r in range(rows)], axis=0
        )
        line_ref[slot + 3] = attended + own_weight * new_value
        context = jnp.concatenate(
            [line_ref[slot + 3, pl.ds(h, rows, stride=group), :] for h in range(group)], axis=1
        ).astype(BF16)
        context_ref[:, columns] = context
    store_blocks(packed_refs, dot(send, context_ref[...]))


def output_up_body(mine_ref, other_ref, uo_ref, *out_refs):
    total = (mine_ref[...] + other_ref[...]).astype(BF16)
    store_blocks(out_refs, ADAPTER_SCALE * dot(total, uo_ref[0]))


def unpack_body(home_ref, ret_refs, out_hbm, out_ref, sems):
    rows, width = out_ref.shape
    home = home_ref[...]
    returned = joined(ret_refs)
    parts = sems.shape[0]
    part = width // parts
    leaving = []
    for i in range(parts):
        columns = slice(i * part, (i + 1) * part)
        out_ref[:, columns] = dot(home, returned[:, columns]).astype(BF16)
        copy = pltpu.make_async_copy(out_ref.at[:, columns], out_hbm.at[:, columns], sems.at[i])
        copy.start()
        leaving.append(copy)
    for copy in leaving:
        copy.wait()


def exchange(blocks, wide_count):
    if len(blocks) == 1:
        slots, width = blocks[0].shape
        moved = lax.all_to_all(
            blocks[0].reshape(wide_count, slots // wide_count, width), "wide", split_axis=0, concat_axis=0, tiled=True
        )
        return (moved.reshape(slots, width),)
    moved = [
        lax.ppermute(block, "wide", [(k, k ^ d) for k in range(wide_count)])
        for d, block in zip(distances(wide_count), blocks[:-1])
    ]
    return (*moved, blocks[-1])


def other_core(value):
    return lax.ppermute(value, "tp", [(0, 1), (1, 0)])


def shards(
    normed_layer_input,
    plain_query_rows,
    plain_key_rows,
    plain_value_rows,
    cached_key_rows,
    cached_value_rows,
    live_cache_length,
    tenant,
    slot_of_adapter,
    stacked_down_weight,
    query_up_weight,
    key_value_up_weight,
    output_down_weight,
    output_up_weight,
):
    wide_count = lax.axis_size("wide")
    rows, features = normed_layer_input.shape
    half = features // lax.axis_size("tp")
    capacity = max(2, 2 * rows // wide_count)
    slots = wide_count * capacity
    kv_heads, cache_size, head_dim = cached_key_rows.shape[1:]
    query_width = plain_query_rows.shape[1]
    group = query_width // head_dim // kv_heads
    lines = rows * group
    by_distance = wide_count <= 8 and wide_count & (wide_count - 1) == 0
    count = wide_count if by_distance else 1
    struct = jax.ShapeDtypeStruct

    def blocks_of(width):
        return [struct((slots // count, width), BF16)] * count


    table, *packed = call(
        functools.partial(pack_body, capacity, by_distance),
        (struct((2, rows), jnp.int32), *blocks_of(half)),
        [HBM] * 4,
        scratch=[
            pltpu.SMEM(tenant.shape, jnp.int32),
            pltpu.SMEM(slot_of_adapter.shape, jnp.int32),
            pltpu.SMEM((rows,), jnp.int32),
            pltpu.VMEM((rows, half), BF16),
            DMA((4,)),
        ],
        flops=10**9,
        moved=40000000,
    )(tenant, slot_of_adapter, live_cache_length, normed_layer_input)
    received = exchange(packed, wide_count)
    prepared = (
        struct((lines, cache_size), F32),
        struct((rows, slots), BF16),
        struct((slots, rows), BF16),
        struct((rows, slots), BF16),
    )
    prepared = call(
        functools.partial(prep_body, group), prepared, [VMEM], flops=10**9, moved=20000000, limit=16
    )(table)
    received, prepared = lax.optimization_barrier((received, prepared))
    rank_part = call(
        down_body, struct((slots, stacked_down_weight.shape[1]), F32), [(VMEM,) * count, VMEM], moved=4000000, limit=16
    )(received, stacked_down_weight)
    rank_other = other_core(rank_part)
    home = prepared[3]
    terms = call(
        functools.partial(up_body, group),
        blocks_of(kv_heads * (group + 2) * head_dim),
        [VMEM] * 4,
        moved=20000000,
        flops=10**9,
        limit=16,
    )(rank_part, rank_other, query_up_weight, key_value_up_weight)
    returned = exchange(terms, wide_count)
    *outgoing, context = call(
        functools.partial(attend_body, group),
        [*blocks_of(query_width), struct((rows, query_width), BF16)],
        [(VMEM,) * count] + [VMEM] * (5 + len(prepared)),
        scratch=[
            pltpu.VMEM((rows, kv_heads * (group + 2) * head_dim), F32),
            pltpu.VMEM((4 * kv_heads, lines, head_dim), F32),
        ],
        moved=8000000,
        limit=16,
    )(
        returned, cached_key_rows, cached_value_rows, plain_query_rows, plain_key_rows, plain_value_rows, *prepared
    )
    arrived = exchange(outgoing, wide_count)
    rank_o = call(
        output_down_body, struct((slots, output_down_weight.shape[1]), F32), [(VMEM,) * count, VMEM], moved=4000000, limit=16
    )(arrived, output_down_weight)
    out_terms = call(
        output_up_body, blocks_of(query_width), [VMEM] * 3, moved=1200000, limit=16
    )(rank_o, other_core(rank_o), output_up_weight)
    adapter_output_term = call(
        unpack_body, struct((rows, query_width), BF16), [VMEM, (VMEM,) * count], HBM,
        scratch=[pltpu.VMEM((rows, query_width), BF16), DMA((4,))], moved=1000000, limit=16,
    )(home, exchange(out_terms, wide_count))
    return context, adapter_output_term


def solution(mesh):
    return jax.shard_map(
        shards,
        mesh=mesh,
        in_specs=(
            P(("groups", "wide"), None),
            P(("groups", "wide"), "tp"),
            P(("groups", "wide"), "tp"),
            P(("groups", "wide"), "tp"),
            P(("groups", "wide"), "tp", None, None),
            P(("groups", "wide"), "tp", None, None),
            P(("groups", "wide")),
            P("groups"),
            P("groups"),
            P("wide", None, None),
            P("wide", None, "tp"),
            P("wide", None, None, "tp"),
            P("wide", None, "tp"),
            P("wide", None, "tp"),
        ),
        out_specs=(P(("groups", "wide"), "tp"), P(("groups", "wide"), "tp")),
        check_vma=False,
    )
```
